512 devices in a mesh: dp: 128 (over z, y, core), rep: 4 (over x).
Axes of the slice: x: 4, y: 4, z: 16, core: 2. Of those that a mesh axis runs over, the one named last changes fastest.
Arguments:
- queries: bfloat16 [131072, 1024], P(('dp', 'rep')), may hold values from -24 to 24
- passages: bfloat16 [16384, 1024], P('dp'), may hold values from -24 to 24
- group_topic: int32 [128], replicated, may hold values from 0 to 15
- topic_rows: int32 [16, 1024], replicated, may hold values from 0 to 16383, as said below
- positive: int32 [131072], P(('dp', 'rep')), may hold values from 0 to 1023
Outputs:
- query_loss: float32 [131072], P(('dp', 'rep'))
- query_grad: bfloat16 [131072, 1024], P(('dp', 'rep'))
- passage_grad: bfloat16 [16384, 1024], P('dp')
The draws below stay inside these ranges and needn't reach their ends.
Inputs may be any that keep to these rules, and one draw needn't show every extreme that they name: `topic_rows`: row t lists the 1024 passages of topic t; its entries k * 8 to (k + 1) * 8 - 1 are passages of rows k * 128 to (k + 1) * 128 - 1; every passage appears exactly once in the table.
All inputs are finite; a program needn't handle non-finite values.
Results may differ from the reference program's by a relative error of at most 0.0046.
Values may be sent and summed in bfloat16 or wider, within the bound.
A program may use at most 64 MiB of HBM per device.

```python
import math
import jax
import jax.numpy as jnp
import numpy as np
from jax import lax

D = 1024
Q_DEV = 256
PASS_DEV = 128
TOPIC_PASS = 1024
TP_DEV = 8
NTOPICS = 16
QUERIES = 131072
PASSAGES = 16384
N_DP = 128
N_REP = 4


def embed_rows(key, rows, salt):
    key = jax.random.fold_in(key, salt)
    first = jax.random.fold_in(key, 0)
    values = jnp.clip(jax.random.normal(first, (rows, D), jnp.float32), -6.0, 6.0)
    return values.astype(jnp.bfloat16)


def draw_queries(key, part):
    return embed_rows(key, QUERIES, 7)


def draw_passages(key, part):
    return embed_rows(key, PASSAGES, 9)


def draw_topic_rows(key, part):
    key = jax.random.fold_in(key, 5)
    owners = PASSAGES // PASS_DEV
    keys = jax.random.split(key, owners)
    orders = jax.vmap(lambda single: jax.random.permutation(single, PASS_DEV))(keys).astype(jnp.int32)
    orders = orders + (jnp.arange(owners, dtype=jnp.int32) * PASS_DEV)[:, None]
    orders = orders.reshape(owners, NTOPICS, TP_DEV).transpose(1, 0, 2)
    return orders.reshape(NTOPICS, TOPIC_PASS)


def touch_ends(values, key, low, largest):
    dims = values.shape
    index_at = [jax.random.randint(jax.random.fold_in(key, axis), (), 0, dims[axis]) for axis in range(len(dims))]
    values = values.at[tuple(index_at)].set(low)
    longest = dims.index(max(dims))
    index_at[longest] = (index_at[longest] + 1) % dims[longest]
    return values.at[tuple(index_at)].set(largest)


def cumulative_ranks(count, slope):
    loads = [(1 << 20) // math.isqrt(standing ** slope) + 1 for standing in range(1, count + 1)]
    scale = 1 + sum(loads) // (1 << 30)
    return np.cumsum(np.array([max(1, weight // scale) for weight in loads]))


def ranked_ids(key, dims, count, lean):
    grid = cumulative_ranks(count, lean)
    pick = jax.random.randint(jax.random.fold_in(key, 1), dims, 0, int(grid[count - 1]))
    standing = jnp.searchsorted(jnp.asarray(grid, jnp.int32), pick, side="right")
    return jax.random.permutation(jax.random.fold_in(key, 2), count)[standing].astype(jnp.int32)


def setup_inputs(seed: int = 0) -> dict:
    key_of = jax.random.split(jax.random.key(seed), 6)
    return {
        "queries": draw_queries(jax.random.fold_in(key_of[5], 71), 0),
        "passages": draw_passages(jax.random.fold_in(key_of[5], 71), 0),
        "group_topic": touch_ends(ranked_ids(key_of[2], (N_DP,), NTOPICS, 2), jax.random.fold_in(key_of[2], 3), 0, NTOPICS - 1).astype(jnp.int32),
        "topic_rows": draw_topic_rows(jax.random.fold_in(key_of[5], 71), 0),
        "positive": touch_ends(jax.random.randint(key_of[4], (QUERIES,), 0, TOPIC_PASS), jax.random.fold_in(key_of[4], 1), 0, TOPIC_PASS - 1).astype(jnp.int32),
    }


def reference(queries, passages, group_topic, topic_rows, positive):
    group_size = Q_DEV * N_REP
    n_groups = QUERIES // group_size
    grouped = queries.reshape(n_groups, group_size, D)
    chosen_all = positive.reshape(n_groups, group_size)
    score_scale = D ** -0.5

    def one_group(total, inputs):
        block, chosen, topic_id = inputs
        listed = topic_rows[topic_id]
        picked = jnp.take(passages, listed, axis=0)
        scores = jnp.dot(block, picked.T, preferred_element_type=jnp.float32) * score_scale
        top_score = jnp.max(scores, axis=1, keepdims=True)
        lse = top_score + jnp.log(jnp.sum(jnp.exp(scores - top_score), axis=1, keepdims=True))
        onehot = jnp.arange(TOPIC_PASS, dtype=jnp.int32)[None, :] == chosen[:, None]
        loss = lse[:, 0] - jnp.sum(jnp.where(onehot, scores, jnp.float32(0.0)), axis=1)
        weights = (jnp.exp(scores - lse) - onehot.astype(jnp.float32)).astype(jnp.bfloat16)
        grad_rows = jnp.dot(weights, picked, preferred_element_type=jnp.float32).astype(jnp.bfloat16)
        grad_term = jnp.dot(weights.T, block, preferred_element_type=jnp.float32)
        total = total.at[listed].add(grad_term)
        return total, (loss, grad_rows)

    start_total = jnp.zeros((PASSAGES, D), jnp.float32)
    total, (losses, grads) = lax.scan(one_group, start_total, (grouped, chosen_all, group_topic))
    return losses.reshape(QUERIES), grads.reshape(QUERIES, D), total.astype(jnp.bfloat16)
```

```python
import jax
import jax.numpy as jnp
from jax import lax
from jax.experimental import pallas as pl
from jax.experimental.pallas import tpu as pltpu
from jax.sharding import PartitionSpec as P

F32, BF16, I32 = jnp.float32, jnp.bfloat16, jnp.int32
MESH = pl.DeviceIdType.MESH
D = 1024
Q = 256
OWN = 128
TOPICS = 16
NZ, NE, NX = 16, 8, 4
SHARE = 2
BLOCK = SHARE * TOPICS
HALF = 128
PARTS = 2
PIECES, PIECE = 4, 32
Q_PACE = (4, 2, 2, 2, 2)
RS_PACE = (4, 4, 4)

STEP = {}
for side in (-1, 1):
    for r in (1, 2, 6, 7):
        STEP[side * r] = side
    for r in (3, 4):
        STEP[side * r] = -side
    STEP[side * 5] = 5 * side
ORDER = (0, -1, 1, -5, 5, -2, 2, -4, 4, -6, 6, -3, 3, -7, 7, 8)
SLOT = {r: n for n, r in enumerate(ORDER)}


def sources(r, i):
    if r == 8:
        return (-1, -7) if i == 0 else (1, 7)
    return STEP[r], r - STEP[r]


CHILDREN = {
    (r, i): [c for c in ORDER if c and sources(c, i)[1] == r] for r in ORDER for i in range(PARTS)
}


def dot(a, b, contract=(1, 0)):
    dims = (((contract[0],), (contract[1],)), ((), ()))
    return lax.dot_general(a, b, dims, preferred_element_type=F32)


def kernel(
    q_ref, p_ref, gt_ref, rows_ref, pos_ref,
    loss_ref, qg_ref, pg_ref,
    loss_v, qg_v, pg_v, pass_here, rows_here, topics, qall, posall, mat, mat_t, smat, smat_t, zbuf, ysend, picked,
    st, part, stats, row, wt,
    gsend, grecv, qpart, rssend, rsrecv, table, bsend, brecv, fin,
    local_sem, q_s, q_r, pos_s, pos_r, z_s, z_r, y_s, y_r,
    stat_s, stat_r, rs_s, rs_r, g_s, g_r, b_s, b_r, fin_s, fin_r,
):
    dp = lax.axis_index("dp")
    x = lax.axis_index("rep")
    z, e = dp // NE, dp % NE
    zs = {d: (lax.rem(z + d + NZ, NZ) * NE + e, x) for d in (-5, -1, 1, 5)}
    x_at = [lax.rem(x + o, NX) for o in range(NX)]
    e_at = [lax.rem(e + o, NE) for o in range(NE)]
    xs = [(dp, x_at[o]) for o in range(NX)]
    es = [(z * NE + e_at[o], x) for o in range(NE)]
    x_up, x_down = xs[1], xs[NX - 1]

    barrier = pltpu.get_barrier_semaphore()
    partners = list(zs.values()) + xs[1:] + es[1:]
    for partner in partners:
        pl.semaphore_signal(barrier, inc=1, device_id=partner, device_id_type=MESH)

    block = pl.ds(pl.multiple_of((dp // 16) * 128, 128), 128)
    loads = [
        pltpu.make_async_copy(src, dst, local_sem.at[n])
        for n, (src, dst) in enumerate(
            (
                (rows_ref.at[:, block], rows_here),
                (p_ref, pass_here),
                (gt_ref, topics),
                (q_ref, qall.at[x]),
                (pos_ref, posall.at[x]),
            )
        )
    ]
    for load in loads:
        load.start()

    started = []

    def send(src, dst, send_sem, recv_sem, to):
        copy = pltpu.make_async_remote_copy(
            src_ref=src, dst_ref=dst, send_sem=send_sem, recv_sem=recv_sem,
            device_id=to, device_id_type=MESH,
        )
        copy.start()
        started.append(copy)
        return copy

    def finish_sends():
        while started:
            started.pop(0).wait_send()

    lane = lax.broadcasted_iota(I32, (TOPICS, OWN), 1)
    first = (dp % 16) * 8
    loads[0].wait()
    here = rows_here[...] - dp * OWN
    for i in range(8):
        col = jnp.sum(jnp.where(lane == first + i, here, 0).astype(F32), axis=1, keepdims=True)
        mat[i * 16 : (i + 1) * 16, :] = jnp.where(lane.astype(F32) == col, 1.0, 0.0).astype(BF16)
    mine = mat[pl.ds(pl.multiple_of(x * BLOCK, BLOCK), BLOCK), :]
    loads[1].wait()
    zbuf[0] = dot(mine, pass_here[...]).astype(BF16)
    for load in loads[2:]:
        load.wait()

    pl.semaphore_wait(barrier, len(partners))

    def sub(i):
        return pl.ds(i * (BLOCK // PARTS), BLOCK // PARTS)

    zc = {}

    def spread(r, i):
        for c in CHILDREN[r, i]:
            n = SLOT[c]
            zc[c, i] = send(
                zbuf.at[SLOT[r], sub(i)], zbuf.at[n, sub(i)],
                z_s.at[n, i], z_r.at[n, i], zs[-sources(c, i)[0]],
            )

    for i in range(PARTS):
        spread(0, i)

    qc, seen = {}, set()

    def got(copies, *keys):
        for key in keys:
            if (id(copies), key) not in seen:
                seen.add((id(copies), key))
                copies[key].wait_recv()

    def send_q(way, n):
        stage, i = divmod(n, PIECES)
        half = way if stage != 1 else 1 - way
        owner = x
        if stage == 2:
            owner = x_at[1] if way else x_at[3]
            got(qc, (way, i))
        rows = qall.at[owner, pl.ds(half * HALF + i * PIECE, PIECE)]
        qc[way, n] = send(rows, rows, q_s.at[way, n], q_r.at[way, n], x_down if way else x_up)

    def paced(send_piece, pace, h):
        for n in range(sum(pace[:h]), sum(pace[: h + 1])):
            send_piece(0, n)
            send_piece(1, n)

    paced(send_q, Q_PACE, 0)

    r16 = lax.broadcasted_iota(I32, (16, 256), 0)
    c256 = lax.broadcasted_iota(I32, (16, 256), 1)
    at = (r16 // 2) * BLOCK + (r16 % 2) * TOPICS
    for d in range(NE):
        chosen = at + topics[z * NE + d]
        smat[d * 16 : (d + 1) * 16, :] = jnp.where(c256 == chosen, 1.0, 0.0).astype(BF16)
    smat_t[...] = smat[...].T
    mat_t[...] = mat[...].T

    yc = {}

    def pick(ch):
        blocks = zbuf[ch * 8 : (ch + 1) * 8].reshape(256, D)
        ysend[ch] = dot(smat[...], blocks).astype(BF16).reshape(NE, 16, D)
        for o in range(1, NE):
            yc[ch, o] = send(
                ysend.at[ch, e_at[o]], picked.at[ch, e],
                y_s.at[ch, o - 1], y_r.at[ch, o - 1], es[o],
            )
        picked[ch, e] = ysend[ch, e]

    def receive(*distances):
        for i in range(PARTS):
            for r in distances:
                zc[r, i].wait_recv()
                spread(r, i)

    receive(-1, 1)
    paced(send_q, Q_PACE, 1)
    pos_c = [
        send(posall.at[x], posall.at[x], pos_s.at[o - 1], pos_r.at[o - 1], xs[o])
        for o in range(1, NX)
    ]
    receive(-5, 5)
    paced(send_q, Q_PACE, 2)
    receive(-2, 2, -4, 4, -6, 6)
    paced(send_q, Q_PACE, 3)
    pick(0)
    paced(send_q, Q_PACE, 4)
    receive(-3, 3, -7, 7)
    receive(8)
    pick(1)

    p = lax.broadcasted_iota(I32, (128, 1), 0)
    listed_at = []
    for ch in range(2):
        away = jnp.zeros((128, 1), I32)
        for n in range(8):
            away = jnp.where((p // 2) % 8 == n, ORDER[ch * 8 + n], away)
        z_of = (z + away + NZ) % NZ
        listed_at.append(z_of * 64 + (p // 16) * 8 + x * SHARE + p % 2)

    def columns(n):
        return pl.ds(pl.multiple_of(n * Q, Q), Q)

    def score(ch, n):
        cols = columns(n)
        s = dot(picked[ch].reshape(128, D), qall[n], (1, 1)) * (D ** -0.5)
        st[ch, :, cols] = s
        top = jnp.max(s, axis=0, keepdims=True)
        part[ch, 0:1, cols] = top
        part[ch, 1:2, cols] = jnp.sum(jnp.exp(s - top), axis=0, keepdims=True)
        hot = listed_at[ch] == posall[n]
        part[ch, 2:3, cols] = jnp.sum(jnp.where(hot, s, 0.0), axis=0, keepdims=True)

    for copy in pos_c:
        copy.wait_recv()
    for o in range(1, NE):
        yc[0, o].wait_recv()
    score(0, x_at[0])
    got(qc, *((0, n) for n in range(2 * PIECES)))
    score(0, x_at[3])
    got(qc, *((1, n) for n in range(2 * PIECES)))
    score(0, x_at[1])
    for o in range(1, NE):
        yc[1, o].wait_recv()
    for o in (0, 3, 1):
        score(1, x_at[o])
    got(qc, *((way, n) for way in range(2) for n in range(2 * PIECES, 3 * PIECES)))
    score(0, x_at[2])
    score(1, x_at[2])

    def merge(pieces):
        top = pieces[0][0]
        for piece in pieces[1:]:
            top = jnp.maximum(top, piece[0])
        total = sum(piece[1] * jnp.exp(piece[0] - top) for piece in pieces)
        return top, total, sum(piece[2] for piece in pieces)

    def rows_of(ref, n):
        return ref[n, 0:1, :], ref[n, 1:2, :], ref[n, 2:3, :]

    top, total, hit = merge([rows_of(part, ch) for ch in range(2)])
    r8 = lax.broadcasted_iota(I32, (8, NX * Q), 0)
    stats[x] = jnp.where(r8 == 0, top, jnp.where(r8 == 1, total, hit))
    finish_fwd = list(started)
    started.clear()
    stat_c = [
        send(stats.at[x], stats.at[x], stat_s.at[o - 1], stat_r.at[o - 1], xs[o])
        for o in range(1, NX)
    ]
    for copy in finish_fwd:
        copy.wait_send()
    for copy in stat_c:
        copy.wait_recv()
    top, total, hit = merge([rows_of(stats, n) for n in range(NX)])
    lse = top + jnp.log(total)
    row[0:1, :] = lse
    row[1:2, :] = lse - hit
    loss_v[...] = row[1:2, columns(x)]
    stores = [pltpu.make_async_copy(loss_v.at[0], loss_ref, local_sem.at[5])]
    stores[0].start()

    for ch in range(2):
        for n in range(NX):
            cols = pl.ds(n * Q, Q)
            hot = jnp.where(listed_at[ch] == posall[n], 1.0, 0.0)
            w = jnp.exp(st[ch, :, cols] - row[0:1, cols]) - hot
            wt[ch * 128 : (ch + 1) * 128, cols] = w.astype(BF16)

    def term(n, _):
        cols = pl.ds(pl.multiple_of(n * 256, 256), 256)
        g = dot(wt[...], qall[:, :, cols].reshape(NX * Q, 256))
        gsend[:, :, :, cols] = g.astype(BF16).reshape(2, NE, 16, 256)
        return 0

    lax.fori_loop(0, D // 256, term, 0)
    gc = {}
    for c in (1, 0):
        for o in range(1, NE):
            gc[c, o] = send(
                gsend.at[c, e_at[o]], grecv.at[c, e],
                g_s.at[c, o - 1], g_r.at[c, o - 1], es[o],
            )
        grecv[c, e] = gsend[c, e]

    def query_part(o):
        w = wt[:, columns(x_at[o])].T

        def tile(n, _):
            out = pl.ds(pl.multiple_of(n * 256, 256), 256)
            qpart[o, :, out] = dot(w, picked[:, :, :, out].reshape(256, 256))
            return 0

        lax.fori_loop(0, D // 256, tile, 0)

    rs = {}

    def send_rs(way, n):
        stage, i = divmod(n, PIECES)
        half = way if stage == 1 else 1 - way
        rows = pl.ds(i * PIECE, PIECE)
        value = qpart[2 if stage == 0 else 3 if way else 1, pl.ds(half * HALF + i * PIECE, PIECE)]
        if stage == 2:
            got(rs, (way, i))
            value = value + rsrecv[way, 0, rows].astype(F32)
        rssend[way, stage, rows] = value.astype(BF16)
        rs[way, n] = send(
            rssend.at[way, stage, rows], rsrecv.at[way, stage, rows],
            rs_s.at[way, n], rs_r.at[way, n], x_down if way else x_up,
        )

    query_part(2)
    paced(send_rs, RS_PACE, 0)
    query_part(1)
    query_part(3)

    def sum_by_topic(c):
        for o in range(1, NE):
            gc[c, o].wait_recv()
        sums = dot(smat_t[...], grecv[c].reshape(128, D))
        table[c * 8 : (c + 1) * 8] = sums.reshape(8, BLOCK, D)

    paced(send_rs, RS_PACE, 1)
    sum_by_topic(1)
    bc = {}

    def summed(r, i):
        value = table[SLOT[r], sub(i)]
        for c in CHILDREN[r, i]:
            bc[c, i].wait_recv()
            value = value + brecv[SLOT[c], sub(i)].astype(F32)
        return value.astype(BF16)

    def send_back(*distances):
        for i in range(PARTS):
            for r in distances:
                n = SLOT[r]
                bsend[n, sub(i)] = summed(r, i)
                bc[r, i] = send(
                    bsend.at[n, sub(i)], brecv.at[n, sub(i)],
                    b_s.at[n, i], b_r.at[n, i], zs[sources(r, i)[0]],
                )

    send_back(8, -3, 3)
    sum_by_topic(0)
    send_back(-7, 7)
    send_back(-4, 4, -2, 2, -6, 6)
    paced(send_rs, RS_PACE, 2)
    send_back(-5, 5, -1, 1)
    fin_c = []
    for i in range(PARTS):
        fin[x, sub(i)] = summed(0, i)
        for o in range(1, NX):
            rows = fin.at[x, sub(i)]
            fin_c.append(send(rows, rows, fin_s.at[o - 1, i], fin_r.at[o - 1, i], xs[o]))
    query_part(0)
    got(rs, *((way, n) for n in range(PIECES, 3 * PIECES) for way in range(2)))
    for half in range(2):
        rows = pl.ds(half * HALF, HALF)
        value = qpart[0, rows] + rsrecv[half, 1].astype(F32) + rsrecv[1 - half, 2].astype(F32)
        qg_v[rows] = value.astype(BF16)
    stores.append(pltpu.make_async_copy(qg_v, qg_ref, local_sem.at[6]))
    stores[1].start()
    for copy in fin_c:
        copy.wait_recv()
    pg_v[...] = dot(mat_t[...], fin[...].reshape(OWN, D)).astype(BF16)
    stores.append(pltpu.make_async_copy(pg_v, pg_ref, local_sem.at[7]))
    stores[2].start()
    finish_sends()
    for store in stores:
        store.wait()


def shards(queries, passages, group_topic, topic_rows, positive):
    hbm = pl.BlockSpec(memory_space=pltpu.HBM)
    dma = pltpu.SemaphoreType.DMA
    loss, query_grad, passage_grad = pl.pallas_call(
        kernel,
        out_shape=(
            jax.ShapeDtypeStruct((Q,), F32),
            jax.ShapeDtypeStruct((Q, D), BF16),
            jax.ShapeDtypeStruct((OWN, D), BF16),
        ),
        in_specs=[hbm] * 5,
        out_specs=(hbm, hbm, hbm),
        scratch_shapes=[
            pltpu.VMEM((1, Q), F32),
            pltpu.VMEM((Q, D), BF16),
            pltpu.VMEM((OWN, D), BF16),
            pltpu.VMEM((OWN, D), BF16),
            pltpu.VMEM((TOPICS, 128), I32),
            pltpu.SMEM((128,), I32),
            pltpu.VMEM((NX, Q, D), BF16),
            pltpu.VMEM((NX, 1, Q), I32),
            pltpu.VMEM((OWN, OWN), BF16),
            pltpu.VMEM((OWN, OWN), BF16),
            pltpu.VMEM((128, 256), BF16),
            pltpu.VMEM((256, 128), BF16),
            pltpu.VMEM((NZ, BLOCK, D), BF16),
            pltpu.VMEM((2, NE, 16, D), BF16),
            pltpu.VMEM((2, NE, 16, D), BF16),
            pltpu.VMEM((2, 128, NX * Q), F32),
            pltpu.VMEM((2, 8, NX * Q), F32),
            pltpu.VMEM((NX, 8, NX * Q), F32),
            pltpu.VMEM((8, NX * Q), F32),
            pltpu.VMEM((256, NX * Q), BF16),
            pltpu.VMEM((2, NE, 16, D), BF16),
            pltpu.VMEM((2, NE, 16, D), BF16),
            pltpu.VMEM((NX, Q, D), F32),
            pltpu.VMEM((2, 3, HALF, D), BF16),
            pltpu.VMEM((2, 3, HALF, D), BF16),
            pltpu.VMEM((NZ, BLOCK, D), F32),
            pltpu.VMEM((NZ, BLOCK, D), BF16),
            pltpu.VMEM((NZ, BLOCK, D), BF16),
            pltpu.VMEM((NX, BLOCK, D), BF16),
            dma((8,)),
            dma((2, 3 * PIECES)), dma((2, 3 * PIECES)), dma((3,)), dma((3,)),
            dma((NZ, PARTS)), dma((NZ, PARTS)),
            dma((2, NE - 1)), dma((2, NE - 1)),
            dma((3,)), dma((3,)), dma((2, 3 * PIECES)), dma((2, 3 * PIECES)),
            dma((2, NE - 1)), dma((2, NE - 1)),
            dma((NZ, PARTS)), dma((NZ, PARTS)),
            dma((3, PARTS)), dma((3, PARTS)),
        ],
        compiler_params=pltpu.CompilerParams(
            collective_id=0, has_side_effects=True, vmem_limit_bytes=60 * 1024 * 1024
        ),
        cost_estimate=pl.CostEstimate(
            flops=3 * 2 * 256 * 1024 * 1024, bytes_accessed=2 * 1024 * 1024, transcendentals=2 * 256 * 1024
        ),
    )(queries, passages, group_topic, topic_rows, positive.reshape(1, Q))
    return loss, query_grad, passage_grad


def solution(mesh):
    return jax.shard_map(
        shards,
        mesh=mesh,
        in_specs=(P(("dp", "rep"), None), P("dp", None), P(), P(), P(("dp", "rep"))),
        out_specs=(P(("dp", "rep")), P(("dp", "rep"), None), P("dp", None)),
        check_vma=False,
    )
```

```python
import jax
import jax.numpy as jnp
from jax import lax
from jax.experimental import pallas as pl
from jax.experimental.pallas import tpu as pltpu
from jax.sharding import PartitionSpec as P

F32, BF16, I32 = jnp.float32, jnp.bfloat16, jnp.int32
MESH = pl.DeviceIdType.MESH
D = 1024
Q = 256
OWN = 128
TOPICS = 16
NZ, NE, NX = 16, 8, 4
SHARE = 2
BLOCK = SHARE * TOPICS
HALF = 128
PARTS = 4
PIECES, PIECE = 4, 32
Q_PACE = (4, 2, 2, 2, 2)
RS_PACE = (4, 4, 4)

STEP = {}
for side in (-1, 1):
    for r in (1, 2, 6, 7):
        STEP[side * r] = side
    for r in (3, 4):
        STEP[side * r] = -side
    STEP[side * 5] = 5 * side
ORDER = (0, -1, 1, -5, 5, -2, 2, -4, 4, -6, 6, -3, 3, -7, 7, 8)
SLOT = {r: n for n, r in enumerate(ORDER)}


def sources(r, i):
    if r == 8:
        return (-1, -7) if i < PARTS // 2 else (1, 7)
    return STEP[r], r - STEP[r]


CHILDREN = {
    (r, i): [c for c in ORDER if c and sources(c, i)[1] == r] for r in ORDER for i in range(PARTS)
}


def dot(a, b, contract=(1, 0)):
    dims = (((contract[0],), (contract[1],)), ((), ()))
    return lax.dot_general(a, b, dims, preferred_element_type=F32)


def kernel(
    q_ref, p_ref, gt_ref, rows_ref, pos_ref,
    loss_ref, qg_ref, pg_ref,
    loss_v, qg_v, pg_v, pass_here, rows_here, topics, qall, posall, mat, mat_t, smat, smat_t, zbuf, ysend, picked,
    st, part, stats, row, wt,
    gsend, grecv, qpart, rssend, rsrecv, table, bsend, brecv, fin,
    local_sem, q_s, q_r, pos_s, pos_r, z_s, z_r, y_s, y_r,
    stat_s, stat_r, rs_s, rs_r, g_s, g_r, b_s, b_r, fin_s, fin_r,
):
    dp = lax.axis_index("dp")
    x = lax.axis_index("rep")
    z, e = dp // NE, dp % NE
    zs = {d: (lax.rem(z + d + NZ, NZ) * NE + e, x) for d in (-5, -1, 1, 5)}
    x_at = [lax.rem(x + o, NX) for o in range(NX)]
    e_at = [lax.rem(e + o, NE) for o in range(NE)]
    xs = [(dp, x_at[o]) for o in range(NX)]
    es = [(z * NE + e_at[o], x) for o in range(NE)]
    x_up, x_down = xs[1], xs[NX - 1]

    barrier = pltpu.get_barrier_semaphore()
    partners = list(zs.values()) + xs[1:] + es[1:]
    for partner in partners:
        pl.semaphore_signal(barrier, inc=1, device_id=partner, device_id_type=MESH)

    block = pl.ds(pl.multiple_of((dp // 16) * 128, 128), 128)
    loads = [
        pltpu.make_async_copy(src, dst, local_sem.at[n])
        for n, (src, dst) in enumerate(
            (
                (rows_ref.at[:, block], rows_here),
                (p_ref, pass_here),
                (gt_ref, topics),
                (q_ref, qall.at[x]),
                (pos_ref, posall.at[x]),
            )
        )
    ]
    for load in loads:
        load.start()

    started = []

    def send(src, dst, send_sem, recv_sem, to):
        copy = pltpu.make_async_remote_copy(
            src_ref=src, dst_ref=dst, send_sem=send_sem, recv_sem=recv_sem,
            device_id=to, device_id_type=MESH,
        )
        copy.start()
        started.append(copy)
        return copy

    def finish_sends():
        while started:
            started.pop(0).wait_send()

    lane = lax.broadcasted_iota(I32, (TOPICS, OWN), 1)
    first = (dp % 16) * 8
    loads[0].wait()
    here = rows_here[...] - dp * OWN
    for i in range(8):
        col = jnp.sum(jnp.where(lane == first + i, here, 0).astype(F32), axis=1, keepdims=True)
        mat[i * 16 : (i + 1) * 16, :] = jnp.where(lane.astype(F32) == col, 1.0, 0.0).astype(BF16)
    mine = mat[pl.ds(pl.multiple_of(x * BLOCK, BLOCK), BLOCK), :]
    loads[1].wait()
    zbuf[0] = dot(mine, pass_here[...]).astype(BF16)
    for load in loads[2:]:
        load.wait()

    pl.semaphore_wait(barrier, len(partners))

    def sub(n, i):
        return n, pl.ds(i // 2 * 16, 16), pl.ds(i % 2 * 512, 512)

    zc = {}

    def spread(r, i):
        for c in CHILDREN[r, i]:
            n = SLOT[c]
            zc[c, i] = send(
                zbuf.at[sub(SLOT[r], i)], zbuf.at[sub(n, i)],
                z_s.at[n, i], z_r.at[n, i], zs[-sources(c, i)[0]],
            )

    for i in range(PARTS):
        spread(0, i)

    qc, seen = {}, set()

    def got(copies, *keys):
        for key in keys:
            if (id(copies), key) not in seen:
                seen.add((id(copies), key))
                copies[key].wait_recv()

    def send_q(way, n):
        stage, i = divmod(n, PIECES)
        half = way if stage != 1 else 1 - way
        owner = x
        if stage == 2:
            owner = x_at[1] if way else x_at[3]
            got(qc, (way, i))
        rows = qall.at[owner, pl.ds(half * HALF + i * PIECE, PIECE)]
        qc[way, n] = send(rows, rows, q_s.at[way, n], q_r.at[way, n], x_down if way else x_up)

    def paced(send_piece, pace, h):
        for n in range(sum(pace[:h]), sum(pace[: h + 1])):
            send_piece(0, n)
            send_piece(1, n)

    paced(send_q, Q_PACE, 0)

    r16 = lax.broadcasted_iota(I32, (16, 256), 0)
    c256 = lax.broadcasted_iota(I32, (16, 256), 1)
    at = (r16 // 2) * BLOCK + (r16 % 2) * TOPICS
    for d in range(NE):
        chosen = at + topics[z * NE + d]
        smat[d * 16 : (d + 1) * 16, :] = jnp.where(c256 == chosen, 1.0, 0.0).astype(BF16)
    smat_t[...] = smat[...].T
    mat_t[...] = mat[...].T

    yc = {}

    def pick(ch):
        blocks = zbuf[ch * 8 : (ch + 1) * 8].reshape(256, D)
        ysend[ch] = dot(smat[...], blocks).astype(BF16).reshape(NE, 16, D)
        for o in range(1, NE):
            yc[ch, o] = send(
                ysend.at[ch, e_at[o]], picked.at[ch, e],
                y_s.at[ch, o - 1], y_r.at[ch, o - 1], es[o],
            )
        picked[ch, e] = ysend[ch, e]

    def receive(*distances):
        for i in range(PARTS):
            for r in distances:
                zc[r, i].wait_recv()
                spread(r, i)

    receive(-1, 1)
    paced(send_q, Q_PACE, 1)
    pos_c = [
        send(posall.at[x], posall.at[x], pos_s.at[o - 1], pos_r.at[o - 1], xs[o])
        for o in range(1, NX)
    ]
    receive(-5, 5)
    paced(send_q, Q_PACE, 2)
    receive(-2, 2, -4, 4, -6, 6)
    paced(send_q, Q_PACE, 3)
    pick(0)
    paced(send_q, Q_PACE, 4)
    receive(-3, 3, -7, 7)
    receive(8)
    pick(1)

    p = lax.broadcasted_iota(I32, (128, 1), 0)
    listed_at = []
    for ch in range(2):
        away = jnp.zeros((128, 1), I32)
        for n in range(8):
            away = jnp.where((p // 2) % 8 == n, ORDER[ch * 8 + n], away)
        z_of = (z + away + NZ) % NZ
        listed_at.append(z_of * 64 + (p // 16) * 8 + x * SHARE + p % 2)

    def columns(n):
        return pl.ds(pl.multiple_of(n * Q, Q), Q)

    def score(ch, n):
        cols = columns(n)
        s = dot(picked[ch].reshape(128, D), qall[n], (1, 1)) * (D ** -0.5)
        st[ch, :, cols] = s
        top = jnp.max(s, axis=0, keepdims=True)
        total = jnp.sum(jnp.exp(s - top), axis=0, keepdims=True)
        hot = listed_at[ch] == posall[n]
        hit = jnp.sum(jnp.where(hot, s, 0.0), axis=0, keepdims=True)
        for k, value in enumerate((top, total, hit)):
            for h in range(2):
                part[ch, k, pl.ds(n * 2 + h, 1), :] = value[:, h * 128 : (h + 1) * 128]

    for copy in pos_c:
        copy.wait_recv()
    for o in range(1, NE):
        yc[0, o].wait_recv()
    score(0, x_at[0])
    got(qc, *((0, n) for n in range(2 * PIECES)))
    score(0, x_at[3])
    got(qc, *((1, n) for n in range(2 * PIECES)))
    score(0, x_at[1])
    for o in range(1, NE):
        yc[1, o].wait_recv()
    for o in (0, 3, 1):
        score(1, x_at[o])
    got(qc, *((way, n) for way in range(2) for n in range(2 * PIECES, 3 * PIECES)))
    score(0, x_at[2])
    score(1, x_at[2])

    def merge(pieces):
        top = pieces[0][0]
        for piece in pieces[1:]:
            top = jnp.maximum(top, piece[0])
        total = sum(piece[1] * jnp.exp(piece[0] - top) for piece in pieces)
        return top, total, sum(piece[2] for piece in pieces)

    def pieces_of(ref, count):
        return [[ref[n, k] for k in range(3)] for n in range(count)]

    for k, value in enumerate(merge(pieces_of(part, 2))):
        stats[x, k] = value
    finish_fwd = list(started)
    started.clear()
    stat_c = [
        send(stats.at[x], stats.at[x], stat_s.at[o - 1], stat_r.at[o - 1], xs[o])
        for o in range(1, NX)
    ]
    for copy in finish_fwd:
        copy.wait_send()
    for copy in stat_c:
        copy.wait_recv()
    top, total, hit = merge(pieces_of(stats, NX))
    lse = top + jnp.log(total)
    row[0] = lse
    row[1] = lse - hit
    loss_v[...] = row[1, pl.ds(x * 2, 2), :]
    stores = [pltpu.make_async_copy(loss_v, loss_ref, local_sem.at[5])]
    stores[0].start()

    gc = {}
    for ch in (1, 0):
        for n in range(NX):
            cols = pl.ds(n * Q, Q)
            hot = jnp.where(listed_at[ch] == posall[n], 1.0, 0.0)
            lse = jnp.concatenate([row[0, 2 * n : 2 * n + 1, :], row[0, 2 * n + 1 : 2 * n + 2, :]], axis=1)
            wt[ch, :, cols] = (jnp.exp(st[ch, :, cols] - lse) - hot).astype(BF16)

        def term(n, _):
            cols = pl.ds(pl.multiple_of(n * 256, 256), 256)
            g = dot(wt[ch], qall[:, :, cols].reshape(NX * Q, 256))
            gsend[ch, :, :, cols] = g.astype(BF16).reshape(NE, 16, 256)
            return 0

        lax.fori_loop(0, D // 256, term, 0)
        for o in range(1, NE):
            gc[ch, o] = send(
                gsend.at[ch, e_at[o]], grecv.at[ch, e],
                g_s.at[ch, o - 1], g_r.at[ch, o - 1], es[o],
            )
        grecv[ch, e] = gsend[ch, e]

    def query_part(o):
        w = wt[:, :, columns(x_at[o])].reshape(256, Q).T

        def tile(n, _):
            out = pl.ds(pl.multiple_of(n * 256, 256), 256)
            qpart[o, :, out] = dot(w, picked[:, :, :, out].reshape(256, 256))
            return 0

        lax.fori_loop(0, D // 256, tile, 0)

    rs = {}

    def send_rs(way, n):
        stage, i = divmod(n, PIECES)
        half = way if stage == 1 else 1 - way
        rows = pl.ds(i * PIECE, PIECE)
        value = qpart[2 if stage == 0 else 3 if way else 1, pl.ds(half * HALF + i * PIECE, PIECE)]
        if stage == 2:
            got(rs, (way, i))
            value = value + rsrecv[way, 0, rows].astype(F32)
        rssend[way, stage, rows] = value.astype(BF16)
        rs[way, n] = send(
            rssend.at[way, stage, rows], rsrecv.at[way, stage, rows],
            rs_s.at[way, n], rs_r.at[way, n], x_down if way else x_up,
        )

    query_part(2)
    paced(send_rs, RS_PACE, 0)
    query_part(1)
    query_part(3)

    def sum_by_topic(c):
        for o in range(1, NE):
            gc[c, o].wait_recv()
        sums = dot(smat_t[...], grecv[c].reshape(128, D))
        table[c * 8 : (c + 1) * 8] = sums.reshape(8, BLOCK, D)

    paced(send_rs, RS_PACE, 1)
    sum_by_topic(1)
    bc = {}

    def summed(r, i):
        value = table[sub(SLOT[r], i)]
        for c in CHILDREN[r, i]:
            bc[c, i].wait_recv()
            value = value + brecv[sub(SLOT[c], i)].astype(F32)
        return value.astype(BF16)

    def send_back(*distances):
        for i in range(PARTS):
            for r in distances:
                n = SLOT[r]
                bsend[sub(n, i)] = summed(r, i)
                bc[r, i] = send(
                    bsend.at[sub(n, i)], brecv.at[sub(n, i)],
                    b_s.at[n, i], b_r.at[n, i], zs[sources(r, i)[0]],
                )

    send_back(8, -3, 3)
    sum_by_topic(0)
    send_back(-7, 7)
    send_back(-4, 4, -2, 2, -6, 6)
    paced(send_rs, RS_PACE, 2)
    send_back(-5, 5, -1, 1)
    fin_c = []
    for i in range(PARTS):
        fin[sub(x, i)] = summed(0, i)
        for o in range(1, NX):
            rows = fin.at[sub(x, i)]
            fin_c.append(send(rows, rows, fin_s.at[o - 1, i], fin_r.at[o - 1, i], xs[o]))
    query_part(0)
    got(rs, *((way, n) for n in range(PIECES, 3 * PIECES) for way in range(2)))
    for half in range(2):
        rows = pl.ds(half * HALF, HALF)
        value = qpart[0, rows] + rsrecv[half, 1].astype(F32) + rsrecv[1 - half, 2].astype(F32)
        qg_v[rows] = value.astype(BF16)
    stores.append(pltpu.make_async_copy(qg_v, qg_ref, local_sem.at[6]))
    stores[1].start()
    for copy in fin_c:
        copy.wait_recv()
    pg_v[...] = dot(mat_t[...], fin[...].reshape(OWN, D)).astype(BF16)
    stores.append(pltpu.make_async_copy(pg_v, pg_ref, local_sem.at[7]))
    stores[2].start()
    finish_sends()
    for store in stores:
        store.wait()


def shards(queries, passages, group_topic, topic_rows, positive):
    hbm = pl.BlockSpec(memory_space=pltpu.HBM)
    dma = pltpu.SemaphoreType.DMA
    loss, query_grad, passage_grad = pl.pallas_call(
        kernel,
        out_shape=(
            jax.ShapeDtypeStruct((2, 128), F32),
            jax.ShapeDtypeStruct((Q, D), BF16),
            jax.ShapeDtypeStruct((OWN, D), BF16),
        ),
        in_specs=[hbm] * 5,
        out_specs=(hbm, hbm, hbm),
        scratch_shapes=[
            pltpu.VMEM((2, 128), F32),
            pltpu.VMEM((Q, D), BF16),
            pltpu.VMEM((OWN, D), BF16),
            pltpu.VMEM((OWN, D), BF16),
            pltpu.VMEM((TOPICS, 128), I32),
            pltpu.SMEM((128,), I32),
            pltpu.VMEM((NX, Q, D), BF16),
            pltpu.VMEM((NX, 1, Q), I32),
            pltpu.VMEM((OWN, OWN), BF16),
            pltpu.VMEM((OWN, OWN), BF16),
            pltpu.VMEM((128, 256), BF16),
            pltpu.VMEM((256, 128), BF16),
            pltpu.VMEM((NZ, BLOCK, D), BF16),
            pltpu.VMEM((2, NE, 16, D), BF16),
            pltpu.VMEM((2, NE, 16, D), BF16),
            pltpu.VMEM((2, 128, NX * Q), F32),
            pltpu.VMEM((2, 3, 8, 128), F32),
            pltpu.VMEM((NX, 3, 8, 128), F32),
            pltpu.VMEM((2, 8, 128), F32),
            pltpu.VMEM((2, 128, NX * Q), BF16),
            pltpu.VMEM((2, NE, 16, D), BF16),
            pltpu.VMEM((2, NE, 16, D), BF16),
            pltpu.VMEM((NX, Q, D), F32),
            pltpu.VMEM((2, 3, HALF, D), BF16),
            pltpu.VMEM((2, 3, HALF, D), BF16),
            pltpu.VMEM((NZ, BLOCK, D), F32),
            pltpu.VMEM((NZ, BLOCK, D), BF16),
            pltpu.VMEM((NZ, BLOCK, D), BF16),
            pltpu.VMEM((NX, BLOCK, D), BF16),
            dma((8,)),
            dma((2, 3 * PIECES)), dma((2, 3 * PIECES)), dma((3,)), dma((3,)),
            dma((NZ, PARTS)), dma((NZ, PARTS)),
            dma((2, NE - 1)), dma((2, NE - 1)),
            dma((3,)), dma((3,)), dma((2, 3 * PIECES)), dma((2, 3 * PIECES)),
            dma((2, NE - 1)), dma((2, NE - 1)),
            dma((NZ, PARTS)), dma((NZ, PARTS)),
            dma((3, PARTS)), dma((3, PARTS)),
        ],
        compiler_params=pltpu.CompilerParams(
            collective_id=0, has_side_effects=True, vmem_limit_bytes=60 * 1024 * 1024
        ),
        cost_estimate=pl.CostEstimate(
            flops=3 * 2 * 256 * 1024 * 1024, bytes_accessed=2 * 1024 * 1024, transcendentals=2 * 256 * 1024
        ),
    )(queries, passages, group_topic, topic_rows, positive.reshape(1, Q))
    return loss.reshape(Q), query_grad, passage_grad


def solution(mesh):
    return jax.shard_map(
        shards,
        mesh=mesh,
        in_specs=(P(("dp", "rep"), None), P("dp", None), P(), P(), P(("dp", "rep"))),
        out_specs=(P(("dp", "rep")), P(("dp", "rep"), None), P("dp", None)),
        check_vma=False,
    )
```

```python
import jax
import jax.numpy as jnp
from jax import lax
from jax.experimental import pallas as pl
from jax.experimental.pallas import tpu as pltpu
from jax.sharding import PartitionSpec as P

F32, BF16, I32 = jnp.float32, jnp.bfloat16, jnp.int32
MESH = pl.DeviceIdType.MESH
D = 1024
Q = 256
OWN = 128
TOPICS = 16
NZ, NE, NX = 16, 8, 4
SHARE = 2
BLOCK = SHARE * TOPICS
HALF = 128
PARTS = 2
Q_PACE = (1, 1, 1)
PIECES, PIECE = 1, 128

ORDER = (0, -1, -5, 5, 1, -2, -6, 4, -4, 6, 2, -7, 3, -3, 7, 8)
STEPS = (
    ((0, 2, 1, 5), (0, 3, 1, -5), (0, 1, 1, 1), (0, 4, 1, -1)),
    ((1, 5, 3, 1), (2, 8, 3, -1)),
    ((6, 11, 2, 1), (8, 13, 2, -1)),
    ((11, 15, 1, 1), (14, 15, 1, -1)),
)


def parts_of(step, m):
    return (m,) if step == 3 else tuple(range(PARTS))


def dot(a, b, contract=(1, 0)):
    dims = (((contract[0],), (contract[1],)), ((), ()))
    return lax.dot_general(a, b, dims, preferred_element_type=F32)


def kernel(
    q_ref, p_ref, gt_ref, rows_ref, pos_ref,
    loss_ref, qg_ref, pg_ref,
    loss_v, qg_v, pg_v, pass_here, rows_here, topics, qall, posall, mat, mat_t, smat, smat_t, zbuf, ysend, picked,
    st, part, stats, row, wt,
    gsend, grecv, qpart, rssend, rsrecv, table, bsend, brecv, fin,
    local_sem, q_s, q_r, pos_s, pos_r, z_s, z_r, y_s, y_r,
    stat_s, stat_r, rs_s, rs_r, g_s, g_r, b_s, b_r, fin_s, fin_r,
):
    dp = lax.axis_index("dp")
    x = lax.axis_index("rep")
    z, e = dp // NE, dp % NE
    zs = {d: (lax.rem(z + d + NZ, NZ) * NE + e, x) for d in (-5, -1, 1, 5)}
    x_at = [lax.rem(x + o, NX) for o in range(NX)]
    e_at = [lax.rem(e + o, NE) for o in range(NE)]
    xs = [(dp, x_at[o]) for o in range(NX)]
    es = [(z * NE + e_at[o], x) for o in range(NE)]
    x_up, x_down = xs[1], xs[NX - 1]

    barrier = pltpu.get_barrier_semaphore()
    partners = list(zs.values()) + xs[1:] + es[1:]
    for partner in partners:
        pl.semaphore_signal(barrier, inc=1, device_id=partner, device_id_type=MESH)

    block = pl.ds(pl.multiple_of((dp // 16) * 128, 128), 128)
    loads = [
        pltpu.make_async_copy(src, dst, local_sem.at[n])
        for n, (src, dst) in enumerate(
            (
                (rows_ref.at[:, block], rows_here),
                (p_ref, pass_here),
                (gt_ref, topics),
                (q_ref, qall.at[x]),
                (pos_ref, posall.at[x]),
            )
        )
    ]
    for load in loads:
        load.start()

    started = []

    def send(src, dst, send_sem, recv_sem, to):
        copy = pltpu.make_async_remote_copy(
            src_ref=src, dst_ref=dst, send_sem=send_sem, recv_sem=recv_sem,
            device_id=to, device_id_type=MESH,
        )
        copy.start()
        started.append(copy)
        return copy

    def finish_sends():
        while started:
            started.pop(0).wait_send()

    lane = lax.broadcasted_iota(I32, (TOPICS, OWN), 1)
    first = (dp % 16) * 8
    loads[0].wait()
    here = rows_here[...] - dp * OWN
    for i in range(8):
        col = jnp.sum(jnp.where(lane == first + i, here, 0).astype(F32), axis=1, keepdims=True)
        mat[i * 16 : (i + 1) * 16, :] = jnp.where(lane.astype(F32) == col, 1.0, 0.0).astype(BF16)
    mine = mat[pl.ds(pl.multiple_of(x * BLOCK, BLOCK), BLOCK), :]
    loads[1].wait()
    zbuf[0] = dot(mine, pass_here[...]).astype(BF16)
    for load in loads[2:]:
        load.wait()

    pl.semaphore_wait(barrier, len(partners))

    def sub(first, count, i):
        return pl.ds(first, count), pl.ds(i * 16, 16)

    zc = {}

    def spread(step, i):
        for m, (src, dst, count, far) in enumerate(STEPS[step]):
            if i in parts_of(step, m):
                zc[step, m, i] = send(
                    zbuf.at[sub(src, count, i)], zbuf.at[sub(dst, count, i)],
                    z_s.at[dst, i], z_r.at[dst, i], zs[far],
                )

    for i in range(PARTS):
        spread(0, i)

    qc, seen = {}, set()

    def got(copies, *keys):
        for key in keys:
            if (id(copies), key) not in seen:
                seen.add((id(copies), key))
                copies[key].wait_recv()

    def send_q(way, n):
        stage, i = divmod(n, PIECES)
        half = way if stage != 1 else 1 - way
        owner = x
        if stage == 2:
            owner = x_at[1] if way else x_at[3]
            got(qc, (way, i))
        rows = qall.at[owner, pl.ds(half * HALF + i * PIECE, PIECE)]
        qc[way, n] = send(rows, rows, q_s.at[way, n], q_r.at[way, n], x_down if way else x_up)

    def paced(send_piece, pace, h):
        for n in range(sum(pace[:h]), sum(pace[: h + 1])):
            send_piece(0, n)
            send_piece(1, n)

    paced(send_q, Q_PACE, 0)

    r16 = lax.broadcasted_iota(I32, (16, 256), 0)
    c256 = lax.broadcasted_iota(I32, (16, 256), 1)
    at = (r16 // 2) * BLOCK + (r16 % 2) * TOPICS
    for d in range(NE):
        chosen = at + topics[z * NE + d]
        smat[d * 16 : (d + 1) * 16, :] = jnp.where(c256 == chosen, 1.0, 0.0).astype(BF16)
    smat_t[...] = smat[...].T
    mat_t[...] = mat[...].T

    yc = {}

    def pick(ch):
        blocks = zbuf[ch * 8 : (ch + 1) * 8].reshape(256, D)
        ysend[ch] = dot(smat[...], blocks).astype(BF16).reshape(NE, 16, D)
        for o in range(1, NE):
            yc[ch, o] = send(
                ysend.at[ch, e_at[o]], picked.at[ch, e],
                y_s.at[ch, o - 1], y_r.at[ch, o - 1], es[o],
            )
        picked[ch, e] = ysend[ch, e]

    def receive(step):
        for i in range(PARTS):
            for m in range(len(STEPS[step])):
                if i in parts_of(step, m):
                    zc[step, m, i].wait_recv()
            if step < 3:
                spread(step + 1, i)

    receive(0)
    paced(send_q, Q_PACE, 1)
    pos_c = [
        send(posall.at[x], posall.at[x], pos_s.at[o - 1], pos_r.at[o - 1], xs[o])
        for o in range(1, NX)
    ]
    receive(1)
    paced(send_q, Q_PACE, 2)
    pick(0)
    receive(2)
    receive(3)
    pick(1)

    p = lax.broadcasted_iota(I32, (128, 1), 0)
    listed_at = []
    for ch in range(2):
        away = jnp.zeros((128, 1), I32)
        for n in range(8):
            away = jnp.where((p // 2) % 8 == n, ORDER[ch * 8 + n], away)
        z_of = (z + away + NZ) % NZ
        listed_at.append(z_of * 64 + (p // 16) * 8 + x * SHARE + p % 2)

    def columns(n):
        return pl.ds(pl.multiple_of(n * Q, Q), Q)

    def score(ch, n):
        cols = columns(n)
        s = dot(picked[ch].reshape(128, D), qall[n], (1, 1)) * (D ** -0.5)
        st[ch, :, cols] = s
        top = jnp.max(s, axis=0, keepdims=True)
        total = jnp.sum(jnp.exp(s - top), axis=0, keepdims=True)
        hot = listed_at[ch] == posall[n]
        hit = jnp.sum(jnp.where(hot, s, 0.0), axis=0, keepdims=True)
        for k, value in enumerate((top, total, hit)):
            for h in range(2):
                part[ch, k, pl.ds(n * 2 + h, 1), :] = value[:, h * 128 : (h + 1) * 128]

    for copy in pos_c:
        copy.wait_recv()
    for o in range(1, NE):
        yc[0, o].wait_recv()
    score(0, x_at[0])
    got(qc, *((0, n) for n in range(2 * PIECES)))
    score(0, x_at[3])
    got(qc, *((1, n) for n in range(2 * PIECES)))
    score(0, x_at[1])
    for o in range(1, NE):
        yc[1, o].wait_recv()
    for o in (0, 3, 1):
        score(1, x_at[o])
    got(qc, *((way, n) for way in range(2) for n in range(2 * PIECES, 3 * PIECES)))
    score(0, x_at[2])
    score(1, x_at[2])

    def merge(pieces):
        top = pieces[0][0]
        for piece in pieces[1:]:
            top = jnp.maximum(top, piece[0])
        total = sum(piece[1] * jnp.exp(piece[0] - top) for piece in pieces)
        return top, total, sum(piece[2] for piece in pieces)

    def pieces_of(ref, count):
        return [[ref[n, k] for k in range(3)] for n in range(count)]

    for k, value in enumerate(merge(pieces_of(part, 2))):
        stats[x, k] = value
    finish_fwd = list(started)
    started.clear()
    stat_c = [
        send(stats.at[x], stats.at[x], stat_s.at[o - 1], stat_r.at[o - 1], xs[o])
        for o in range(1, NX)
    ]
    for copy in finish_fwd:
        copy.wait_send()
    for copy in stat_c:
        copy.wait_recv()
    top, total, hit = merge(pieces_of(stats, NX))
    lse = top + jnp.log(total)
    row[0] = lse
    row[1] = lse - hit
    loss_v[...] = row[1, pl.ds(x * 2, 2), :]
    stores = [pltpu.make_async_copy(loss_v, loss_ref, local_sem.at[5])]
    stores[0].start()

    gc, rs = {}, {}

    def weigh(ch):
        for n in range(NX):
            cols = pl.ds(n * Q, Q)
            hot = jnp.where(listed_at[ch] == posall[n], 1.0, 0.0)
            lse = jnp.concatenate([row[0, 2 * n : 2 * n + 1, :], row[0, 2 * n + 1 : 2 * n + 2, :]], axis=1)
            wt[ch, :, cols] = (jnp.exp(st[ch, :, cols] - lse) - hot).astype(BF16)

    def term(ch):
        def tile(n, _):
            cols = pl.ds(pl.multiple_of(n * 256, 256), 256)
            g = dot(wt[ch], qall[:, :, cols].reshape(NX * Q, 256))
            gsend[ch, :, :, cols] = g.astype(BF16).reshape(NE, 16, 256)
            return 0

        lax.fori_loop(0, D // 256, tile, 0)
        for o in range(1, NE):
            gc[ch, o] = send(
                gsend.at[ch, e_at[o]], grecv.at[ch, e],
                g_s.at[ch, o - 1], g_r.at[ch, o - 1], es[o],
            )
        grecv[ch, e] = gsend[ch, e]

    def query_part(o):
        w = wt[:, :, columns(x_at[o])].reshape(256, Q).T

        def tile(n, _):
            out = pl.ds(pl.multiple_of(n * 256, 256), 256)
            qpart[o, :, out] = dot(w, picked[:, :, :, out].reshape(256, 256))
            return 0

        lax.fori_loop(0, D // 256, tile, 0)

    def send_rs(way, stage):
        for i in range(PIECES):
            half = way if stage == 1 else 1 - way
            rows = pl.ds(i * PIECE, PIECE)
            value = qpart[2 if stage == 0 else 3 if way else 1, pl.ds(half * HALF + i * PIECE, PIECE)]
            n = stage * PIECES + i
            if stage == 2:
                got(rs, (way, i))
                value = value + rsrecv[way, 0, rows].astype(F32)
            rssend[way, stage, rows] = value.astype(BF16)
            rs[way, n] = send(
                rssend.at[way, stage, rows], rsrecv.at[way, stage, rows],
                rs_s.at[way, n], rs_r.at[way, n], x_down if way else x_up,
            )

    weigh(1)
    term(1)
    weigh(0)
    query_part(2)
    send_rs(0, 0)
    send_rs(1, 0)
    query_part(1)
    send_rs(0, 1)
    query_part(3)
    send_rs(1, 1)
    term(0)

    def sum_by_topic(c):
        for o in range(1, NE):
            gc[c, o].wait_recv()
        sums = dot(smat_t[...], grecv[c].reshape(128, D))
        table[c * 8 : (c + 1) * 8] = sums.reshape(8, BLOCK, D)

    sum_by_topic(1)
    bc = {}

    def summed(first, count, i):
        values = [table[first + n, sub(0, 1, i)[1]] for n in range(count)]
        for step in range(1, 4):
            for m, (src, dst, width, _) in enumerate(STEPS[step]):
                held = [n for n in range(width) if first <= src + n < first + count]
                if held and i in parts_of(step, m):
                    if (step, m, i) not in seen:
                        seen.add((step, m, i))
                        bc[step, m, i].wait_recv()
                    for n in held:
                        more = brecv[dst + n, sub(0, 1, i)[1]].astype(F32)
                        values[src + n - first] = values[src + n - first] + more
        return values

    def send_back(step):
        for i in range(PARTS):
            for m, (_, dst, count, far) in enumerate(STEPS[step]):
                if i in parts_of(step, m):
                    for n, value in enumerate(summed(dst, count, i)):
                        bsend[dst + n, sub(0, 1, i)[1]] = value.astype(BF16)
                    bc[step, m, i] = send(
                        bsend.at[sub(dst, count, i)], brecv.at[sub(dst, count, i)],
                        b_s.at[dst, i], b_r.at[dst, i], zs[-far],
                    )

    send_back(3)
    send_back(2)
    sum_by_topic(0)
    send_rs(0, 2)
    send_rs(1, 2)
    send_back(1)
    send_back(0)
    fin_c = []
    for i in range(PARTS):
        rows = sub(0, 1, i)[1]
        value = table[0, rows]
        for m, (_, dst, _, _) in enumerate(STEPS[0]):
            bc[0, m, i].wait_recv()
            value = value + brecv[dst, rows].astype(F32)
        fin[x, rows] = value.astype(BF16)
        for o in range(1, NX):
            here = fin.at[x, rows]
            fin_c.append(send(here, here, fin_s.at[o - 1, i], fin_r.at[o - 1, i], xs[o]))
    query_part(0)
    got(rs, *((way, n) for n in range(PIECES, 3 * PIECES) for way in range(2)))
    for half in range(2):
        rows = pl.ds(half * HALF, HALF)
        value = qpart[0, rows] + rsrecv[half, 1].astype(F32) + rsrecv[1 - half, 2].astype(F32)
        qg_v[rows] = value.astype(BF16)
    stores.append(pltpu.make_async_copy(qg_v, qg_ref, local_sem.at[6]))
    stores[1].start()
    for copy in fin_c:
        copy.wait_recv()
    pg_v[...] = dot(mat_t[...], fin[...].reshape(OWN, D)).astype(BF16)
    stores.append(pltpu.make_async_copy(pg_v, pg_ref, local_sem.at[7]))
    stores[2].start()
    finish_sends()
    for store in stores:
        store.wait()


def shards(queries, passages, group_topic, topic_rows, positive):
    hbm = pl.BlockSpec(memory_space=pltpu.HBM)
    dma = pltpu.SemaphoreType.DMA
    loss, query_grad, passage_grad = pl.pallas_call(
        kernel,
        out_shape=(
            jax.ShapeDtypeStruct((2, 128), F32),
            jax.ShapeDtypeStruct((Q, D), BF16),
            jax.ShapeDtypeStruct((OWN, D), BF16),
        ),
        in_specs=[hbm] * 5,
        out_specs=(hbm, hbm, hbm),
        scratch_shapes=[
            pltpu.VMEM((2, 128), F32),
            pltpu.VMEM((Q, D), BF16),
            pltpu.VMEM((OWN, D), BF16),
            pltpu.VMEM((OWN, D), BF16),
            pltpu.VMEM((TOPICS, 128), I32),
            pltpu.SMEM((128,), I32),
            pltpu.VMEM((NX, Q, D), BF16),
            pltpu.VMEM((NX, 1, Q), I32),
            pltpu.VMEM((OWN, OWN), BF16),
            pltpu.VMEM((OWN, OWN), BF16),
            pltpu.VMEM((128, 256), BF16),
            pltpu.VMEM((256, 128), BF16),
            pltpu.VMEM((NZ, BLOCK, D), BF16),
            pltpu.VMEM((2, NE, 16, D), BF16),
            pltpu.VMEM((2, NE, 16, D), BF16),
            pltpu.VMEM((2, 128, NX * Q), F32),
            pltpu.VMEM((2, 3, 8, 128), F32),
            pltpu.VMEM((NX, 3, 8, 128), F32),
            pltpu.VMEM((2, 8, 128), F32),
            pltpu.VMEM((2, 128, NX * Q), BF16),
            pltpu.VMEM((2, NE, 16, D), BF16),
            pltpu.VMEM((2, NE, 16, D), BF16),
            pltpu.VMEM((NX, Q, D), F32),
            pltpu.VMEM((2, 3, HALF, D), BF16),
            pltpu.VMEM((2, 3, HALF, D), BF16),
            pltpu.VMEM((NZ, BLOCK, D), F32),
            pltpu.VMEM((NZ, BLOCK, D), BF16),
            pltpu.VMEM((NZ, BLOCK, D), BF16),
            pltpu.VMEM((NX, BLOCK, D), BF16),
            dma((8,)),
            dma((2, 3 * PIECES)), dma((2, 3 * PIECES)), dma((3,)), dma((3,)),
            dma((NZ, PARTS)), dma((NZ, PARTS)),
            dma((2, NE - 1)), dma((2, NE - 1)),
            dma((3,)), dma((3,)), dma((2, 3 * PIECES)), dma((2, 3 * PIECES)),
            dma((2, NE - 1)), dma((2, NE - 1)),
            dma((NZ, PARTS)), dma((NZ, PARTS)),
            dma((3, PARTS)), dma((3, PARTS)),
        ],
        compiler_params=pltpu.CompilerParams(
            collective_id=0, has_side_effects=True, vmem_limit_bytes=60 * 1024 * 1024
        ),
        cost_estimate=pl.CostEstimate(
            flops=3 * 2 * 256 * 1024 * 1024, bytes_accessed=2 * 1024 * 1024, transcendentals=2 * 256 * 1024
        ),
    )(queries, passages, group_topic, topic_rows, positive.reshape(1, Q))
    return loss.reshape(Q), query_grad, passage_grad


def solution(mesh):
    return jax.shard_map(
        shards,
        mesh=mesh,
        in_specs=(P(("dp", "rep"), None), P("dp", None), P(), P(), P(("dp", "rep"))),
        out_specs=(P(("dp", "rep")), P(("dp", "rep"), None), P("dp", None)),
        check_vma=False,
    )
```

```python
import jax
import jax.numpy as jnp
from jax import lax
from jax.experimental import pallas as pl
from jax.experimental.pallas import tpu as pltpu
from jax.sharding import PartitionSpec as P

F32, BF16, I32 = jnp.float32, jnp.bfloat16, jnp.int32
MESH = pl.DeviceIdType.MESH
D = 1024
Q = 256
OWN = 128
TOPICS = 16
NZ, NE, NX = 16, 8, 4
SHARE = 2
BLOCK = SHARE * TOPICS
HALF = 128
PARTS = 2
Q_PACE = (2, 1)
PIECES, PIECE = 1, 128

ORDER = (0, -1, -5, 5, 1, -2, -6, 4, -4, 6, 2, -7, 3, -3, 7, 8)
STEPS = (
    ((0, 2, 1, 5), (0, 3, 1, -5), (0, 1, 1, 1), (0, 4, 1, -1)),
    ((1, 5, 3, 1), (2, 8, 3, -1)),
    ((6, 11, 2, 1), (8, 13, 2, -1)),
    ((11, 15, 1, 1), (14, 15, 1, -1)),
)


def parts_of(step, m):
    return (m,) if step == 3 else tuple(range(PARTS))


def dot(a, b, contract=(1, 0)):
    dims = (((contract[0],), (contract[1],)), ((), ()))
    return lax.dot_general(a, b, dims, preferred_element_type=F32)


def kernel(
    q_ref, p_ref, gt_ref, rows_ref, pos_ref,
    loss_ref, qg_ref, pg_ref,
    loss_v, qg_v, pg_v, pass_here, rows_here, topics, qall, posall, mat, mat_t, smat, smat_t, zbuf, ysend, picked,
    st, part, stats, row, wt,
    gsend, grecv, qpart, rssend, rsrecv, table, bsend, brecv, fin,
    local_sem, q_s, q_r, pos_s, pos_r, z_s, z_r, y_s, y_r,
    stat_s, stat_r, rs_s, rs_r, g_s, g_r, b_s, b_r, fin_s, fin_r,
):
    dp = lax.axis_index("dp")
    x = lax.axis_index("rep")
    z, e = dp // NE, dp % NE
    zs = {d: (lax.rem(z + d + NZ, NZ) * NE + e, x) for d in (-5, -1, 1, 5)}
    x_at = [lax.rem(x + o, NX) for o in range(NX)]
    e_at = [lax.rem(e + o, NE) for o in range(NE)]
    xs = [(dp, x_at[o]) for o in range(NX)]
    es = [(z * NE + e_at[o], x) for o in range(NE)]
    x_up, x_down = xs[1], xs[NX - 1]

    barrier = pltpu.get_barrier_semaphore()
    partners = list(zs.values()) + xs[1:] + es[1:]
    for partner in partners:
        pl.semaphore_signal(barrier, inc=1, device_id=partner, device_id_type=MESH)

    block = pl.ds(pl.multiple_of((dp // 16) * 128, 128), 128)
    loads = [
        pltpu.make_async_copy(src, dst, local_sem.at[n])
        for n, (src, dst) in enumerate(
            (
                (rows_ref.at[:, block], rows_here),
                (p_ref, pass_here),
                (gt_ref, topics),
                (q_ref, qall.at[x]),
                (pos_ref, posall.at[x]),
            )
        )
    ]
    for load in loads:
        load.start()

    started = []

    def send(src, dst, send_sem, recv_sem, to):
        copy = pltpu.make_async_remote_copy(
            src_ref=src, dst_ref=dst, send_sem=send_sem, recv_sem=recv_sem,
            device_id=to, device_id_type=MESH,
        )
        copy.start()
        started.append(copy)
        return copy

    def finish_sends():
        while started:
            started.pop(0).wait_send()

    lane = lax.broadcasted_iota(I32, (TOPICS, OWN), 1)
    first = (dp % 16) * 8
    loads[0].wait()
    here = rows_here[...] - dp * OWN
    for i in range(8):
        col = jnp.sum(jnp.where(lane == first + i, here, 0).astype(F32), axis=1, keepdims=True)
        mat[i * 16 : (i + 1) * 16, :] = jnp.where(lane.astype(F32) == col, 1.0, 0.0).astype(BF16)
    mine = mat[pl.ds(pl.multiple_of(x * BLOCK, BLOCK), BLOCK), :]
    loads[1].wait()
    zbuf[0] = dot(mine, pass_here[...]).astype(BF16)
    for load in loads[2:]:
        load.wait()

    pl.semaphore_wait(barrier, len(partners))

    def sub(first, count, i):
        return pl.ds(first, count), pl.ds(i * 16, 16)

    zc = {}

    def spread(step, i):
        for m, (src, dst, count, far) in enumerate(STEPS[step]):
            if i in parts_of(step, m):
                zc[step, m, i] = send(
                    zbuf.at[sub(src, count, i)], zbuf.at[sub(dst, count, i)],
                    z_s.at[dst, i], z_r.at[dst, i], zs[far],
                )

    for i in range(PARTS):
        spread(0, i)

    qc, seen = {}, set()

    def got(copies, *keys):
        for key in keys:
            if (id(copies), key) not in seen:
                seen.add((id(copies), key))
                copies[key].wait_recv()

    def send_q(way, n):
        stage, i = divmod(n, PIECES)
        half = way if stage != 1 else 1 - way
        owner = x
        if stage == 2:
            owner = x_at[1] if way else x_at[3]
            got(qc, (way, i))
        rows = qall.at[owner, pl.ds(half * HALF + i * PIECE, PIECE)]
        qc[way, n] = send(rows, rows, q_s.at[way, n], q_r.at[way, n], x_down if way else x_up)

    def paced(send_piece, pace, h):
        for n in range(sum(pace[:h]), sum(pace[: h + 1])):
            send_piece(0, n)
            send_piece(1, n)

    paced(send_q, Q_PACE, 0)

    r16 = lax.broadcasted_iota(I32, (16, 256), 0)
    c256 = lax.broadcasted_iota(I32, (16, 256), 1)
    at = (r16 // 2) * BLOCK + (r16 % 2) * TOPICS
    for d in range(NE):
        chosen = at + topics[z * NE + d]
        smat[d * 16 : (d + 1) * 16, :] = jnp.where(c256 == chosen, 1.0, 0.0).astype(BF16)
    smat_t[...] = smat[...].T
    mat_t[...] = mat[...].T

    yc = {}

    def pick(ch):
        blocks = zbuf[ch * 8 : (ch + 1) * 8].reshape(256, D)
        ysend[ch] = dot(smat[...], blocks).astype(BF16).reshape(NE, 16, D)
        for o in range(1, NE):
            yc[ch, o] = send(
                ysend.at[ch, e_at[o]], picked.at[ch, e],
                y_s.at[ch, o - 1], y_r.at[ch, o - 1], es[o],
            )
        picked[ch, e] = ysend[ch, e]

    def receive(step):
        for i in range(PARTS):
            for m in range(len(STEPS[step])):
                if i in parts_of(step, m):
                    zc[step, m, i].wait_recv()
            if step < 3:
                spread(step + 1, i)

    receive(0)
    paced(send_q, Q_PACE, 1)
    pos_c = [
        send(posall.at[x], posall.at[x], pos_s.at[o - 1], pos_r.at[o - 1], xs[o])
        for o in range(1, NX)
    ]
    receive(1)
    pick(0)
    receive(2)
    receive(3)
    pick(1)

    p = lax.broadcasted_iota(I32, (128, 1), 0)
    listed_at = []
    for ch in range(2):
        away = jnp.zeros((128, 1), I32)
        for n in range(8):
            away = jnp.where((p // 2) % 8 == n, ORDER[ch * 8 + n], away)
        z_of = (z + away + NZ) % NZ
        listed_at.append(z_of * 64 + (p // 16) * 8 + x * SHARE + p % 2)

    def columns(n):
        return pl.ds(pl.multiple_of(n * Q, Q), Q)

    def score(ch, n):
        cols = columns(n)
        s = dot(picked[ch].reshape(128, D), qall[n], (1, 1)) * (D ** -0.5)
        st[ch, :, cols] = s
        top = jnp.max(s, axis=0, keepdims=True)
        total = jnp.sum(jnp.exp(s - top), axis=0, keepdims=True)
        hot = listed_at[ch] == posall[n]
        hit = jnp.sum(jnp.where(hot, s, 0.0), axis=0, keepdims=True)
        for k, value in enumerate((top, total, hit)):
            for h in range(2):
                part[ch, k, pl.ds(n * 2 + h, 1), :] = value[:, h * 128 : (h + 1) * 128]

    for copy in pos_c:
        copy.wait_recv()
    for o in range(1, NE):
        yc[0, o].wait_recv()
    score(0, x_at[0])
    got(qc, *((0, n) for n in range(2 * PIECES)))
    score(0, x_at[3])
    got(qc, *((1, n) for n in range(2 * PIECES)))
    score(0, x_at[1])
    for o in range(1, NE):
        yc[1, o].wait_recv()
    for o in (0, 3, 1):
        score(1, x_at[o])
    got(qc, *((way, n) for way in range(2) for n in range(2 * PIECES, 3 * PIECES)))
    score(0, x_at[2])
    score(1, x_at[2])

    def merge(pieces):
        top = pieces[0][0]
        for piece in pieces[1:]:
            top = jnp.maximum(top, piece[0])
        total = sum(piece[1] * jnp.exp(piece[0] - top) for piece in pieces)
        return top, total, sum(piece[2] for piece in pieces)

    def pieces_of(ref, count):
        return [[ref[n, k] for k in range(3)] for n in range(count)]

    for k, value in enumerate(merge(pieces_of(part, 2))):
        stats[x, k] = value
    finish_fwd = list(started)
    started.clear()
    stat_c = [
        send(stats.at[x], stats.at[x], stat_s.at[o - 1], stat_r.at[o - 1], xs[o])
        for o in range(1, NX)
    ]
    for copy in finish_fwd:
        copy.wait_send()
    for copy in stat_c:
        copy.wait_recv()
    top, total, hit = merge(pieces_of(stats, NX))
    lse = top + jnp.log(total)
    row[0] = lse
    row[1] = lse - hit
    loss_v[...] = row[1, pl.ds(x * 2, 2), :]
    stores = [pltpu.make_async_copy(loss_v, loss_ref, local_sem.at[5])]
    stores[0].start()

    gc, rs = {}, {}

    def weigh(ch):
        for n in range(NX):
            cols = pl.ds(n * Q, Q)
            hot = jnp.where(listed_at[ch] == posall[n], 1.0, 0.0)
            lse = jnp.concatenate([row[0, 2 * n : 2 * n + 1, :], row[0, 2 * n + 1 : 2 * n + 2, :]], axis=1)
            wt[ch, :, cols] = (jnp.exp(st[ch, :, cols] - lse) - hot).astype(BF16)

    def term(ch):
        def tile(n, _):
            cols = pl.ds(pl.multiple_of(n * 256, 256), 256)
            g = dot(wt[ch], qall[:, :, cols].reshape(NX * Q, 256))
            gsend[ch, :, :, cols] = g.astype(BF16).reshape(NE, 16, 256)
            return 0

        lax.fori_loop(0, D // 256, tile, 0)
        for o in range(1, NE):
            gc[ch, o] = send(
                gsend.at[ch, e_at[o]], grecv.at[ch, e],
                g_s.at[ch, o - 1], g_r.at[ch, o - 1], es[o],
            )
        grecv[ch, e] = gsend[ch, e]

    def query_part(o):
        w = wt[:, :, columns(x_at[o])].reshape(256, Q).T

        def tile(n, _):
            out = pl.ds(pl.multiple_of(n * 256, 256), 256)
            qpart[o, :, out] = dot(w, picked[:, :, :, out].reshape(256, 256))
            return 0

        lax.fori_loop(0, D // 256, tile, 0)

    def send_rs(way, stage):
        for i in range(PIECES):
            half = way if stage == 1 else 1 - way
            rows = pl.ds(i * PIECE, PIECE)
            value = qpart[2 if stage == 0 else 3 if way else 1, pl.ds(half * HALF + i * PIECE, PIECE)]
            n = stage * PIECES + i
            if stage == 2:
                got(rs, (way, i))
                value = value + rsrecv[way, 0, rows].astype(F32)
            rssend[way, stage, rows] = value.astype(BF16)
            rs[way, n] = send(
                rssend.at[way, stage, rows], rsrecv.at[way, stage, rows],
                rs_s.at[way, n], rs_r.at[way, n], x_down if way else x_up,
            )

    weigh(1)
    weigh(0)
    query_part(2)
    send_rs(0, 0)
    send_rs(1, 0)
    term(1)
    query_part(1)
    send_rs(0, 1)
    query_part(3)
    send_rs(1, 1)
    term(0)

    def sum_by_topic(c):
        for o in range(1, NE):
            gc[c, o].wait_recv()
        sums = dot(smat_t[...], grecv[c].reshape(128, D))
        table[c * 8 : (c + 1) * 8] = sums.reshape(8, BLOCK, D)

    sum_by_topic(1)
    bc = {}

    def summed(first, count, i):
        values = [table[first + n, sub(0, 1, i)[1]] for n in range(count)]
        for step in range(1, 4):
            for m, (src, dst, width, _) in enumerate(STEPS[step]):
                held = [n for n in range(width) if first <= src + n < first + count]
                if held and i in parts_of(step, m):
                    if (step, m, i) not in seen:
                        seen.add((step, m, i))
                        bc[step, m, i].wait_recv()
                    for n in held:
                        more = brecv[dst + n, sub(0, 1, i)[1]].astype(F32)
                        values[src + n - first] = values[src + n - first] + more
        return values

    def send_back(step):
        for i in range(PARTS):
            for m, (_, dst, count, far) in enumerate(STEPS[step]):
                if i in parts_of(step, m):
                    for n, value in enumerate(summed(dst, count, i)):
                        bsend[dst + n, sub(0, 1, i)[1]] = value.astype(BF16)
                    bc[step, m, i] = send(
                        bsend.at[sub(dst, count, i)], brecv.at[sub(dst, count, i)],
                        b_s.at[dst, i], b_r.at[dst, i], zs[-far],
                    )

    send_back(3)
    send_back(2)
    sum_by_topic(0)
    send_rs(0, 2)
    send_rs(1, 2)
    send_back(1)
    send_back(0)
    fin_c = []
    for i in range(PARTS):
        rows = sub(0, 1, i)[1]
        value = table[0, rows]
        for m, (_, dst, _, _) in enumerate(STEPS[0]):
            bc[0, m, i].wait_recv()
            value = value + brecv[dst, rows].astype(F32)
        fin[x, rows] = value.astype(BF16)
        for o in range(1, NX):
            here = fin.at[x, rows]
            fin_c.append(send(here, here, fin_s.at[o - 1, i], fin_r.at[o - 1, i], xs[o]))
    query_part(0)
    got(rs, *((way, n) for n in range(PIECES, 3 * PIECES) for way in range(2)))
    for half in range(2):
        rows = pl.ds(half * HALF, HALF)
        value = qpart[0, rows] + rsrecv[half, 1].astype(F32) + rsrecv[1 - half, 2].astype(F32)
        qg_v[rows] = value.astype(BF16)
    stores.append(pltpu.make_async_copy(qg_v, qg_ref, local_sem.at[6]))
    stores[1].start()
    for copy in fin_c:
        copy.wait_recv()
    pg_v[...] = dot(mat_t[...], fin[...].reshape(OWN, D)).astype(BF16)
    stores.append(pltpu.make_async_copy(pg_v, pg_ref, local_sem.at[7]))
    stores[2].start()
    finish_sends()
    for store in stores:
        store.wait()


def shards(queries, passages, group_topic, topic_rows, positive):
    hbm = pl.BlockSpec(memory_space=pltpu.HBM)
    dma = pltpu.SemaphoreType.DMA
    loss, query_grad, passage_grad = pl.pallas_call(
        kernel,
        out_shape=(
            jax.ShapeDtypeStruct((2, 128), F32),
            jax.ShapeDtypeStruct((Q, D), BF16),
            jax.ShapeDtypeStruct((OWN, D), BF16),
        ),
        in_specs=[hbm] * 5,
        out_specs=(hbm, hbm, hbm),
        scratch_shapes=[
            pltpu.VMEM((2, 128), F32),
            pltpu.VMEM((Q, D), BF16),
            pltpu.VMEM((OWN, D), BF16),
            pltpu.VMEM((OWN, D), BF16),
            pltpu.VMEM((TOPICS, 128), I32),
            pltpu.SMEM((128,), I32),
            pltpu.VMEM((NX, Q, D), BF16),
            pltpu.VMEM((NX, 1, Q), I32),
            pltpu.VMEM((OWN, OWN), BF16),
            pltpu.VMEM((OWN, OWN), BF16),
            pltpu.VMEM((128, 256), BF16),
            pltpu.VMEM((256, 128), BF16),
            pltpu.VMEM((NZ, BLOCK, D), BF16),
            pltpu.VMEM((2, NE, 16, D), BF16),
            pltpu.VMEM((2, NE, 16, D), BF16),
            pltpu.VMEM((2, 128, NX * Q), F32),
            pltpu.VMEM((2, 3, 8, 128), F32),
            pltpu.VMEM((NX, 3, 8, 128), F32),
            pltpu.VMEM((2, 8, 128), F32),
            pltpu.VMEM((2, 128, NX * Q), BF16),
            pltpu.VMEM((2, NE, 16, D), BF16),
            pltpu.VMEM((2, NE, 16, D), BF16),
            pltpu.VMEM((NX, Q, D), F32),
            pltpu.VMEM((2, 3, HALF, D), BF16),
            pltpu.VMEM((2, 3, HALF, D), BF16),
            pltpu.VMEM((NZ, BLOCK, D), F32),
            pltpu.VMEM((NZ, BLOCK, D), BF16),
            pltpu.VMEM((NZ, BLOCK, D), BF16),
            pltpu.VMEM((NX, BLOCK, D), BF16),
            dma((8,)),
            dma((2, 3 * PIECES)), dma((2, 3 * PIECES)), dma((3,)), dma((3,)),
            dma((NZ, PARTS)), dma((NZ, PARTS)),
            dma((2, NE - 1)), dma((2, NE - 1)),
            dma((3,)), dma((3,)), dma((2, 3 * PIECES)), dma((2, 3 * PIECES)),
            dma((2, NE - 1)), dma((2, NE - 1)),
            dma((NZ, PARTS)), dma((NZ, PARTS)),
            dma((3, PARTS)), dma((3, PARTS)),
        ],
        compiler_params=pltpu.CompilerParams(
            collective_id=0, has_side_effects=True, vmem_limit_bytes=60 * 1024 * 1024
        ),
        cost_estimate=pl.CostEstimate(
            flops=3 * 2 * 256 * 1024 * 1024, bytes_accessed=2 * 1024 * 1024, transcendentals=2 * 256 * 1024
        ),
    )(queries, passages, group_topic, topic_rows, positive.reshape(1, Q))
    return loss.reshape(Q), query_grad, passage_grad


def solution(mesh):
    return jax.shard_map(
        shards,
        mesh=mesh,
        in_specs=(P(("dp", "rep"), None), P("dp", None), P(), P(), P(("dp", "rep"))),
        out_specs=(P(("dp", "rep")), P(("dp", "rep"), None), P("dp", None)),
        check_vma=False,
    )
```

```python
import jax
import jax.numpy as jnp
from jax import lax
from jax.experimental import pallas as pl
from jax.experimental.pallas import tpu as pltpu
from jax.sharding import PartitionSpec as P

F32, BF16, I32 = jnp.float32, jnp.bfloat16, jnp.int32
MESH = pl.DeviceIdType.MESH
D = 1024
Q = 256
OWN = 128
TOPICS = 16
NZ, NE, NX = 16, 8, 4
SHARE = 2
BLOCK = SHARE * TOPICS
HALF = 128
FAR_FIRST = (4, 3, 5, 2, 6, 1, 7)
PARTS = 2
Q_PACE = (1, 1, 1)
PIECES, PIECE = 1, 128

ORDER = (0, -1, -5, 5, 1, -2, -6, 4, -4, 6, 2, -7, 3, -3, 7, 8)
STEPS = (
    ((0, 2, 1, 5), (0, 3, 1, -5), (0, 1, 1, 1), (0, 4, 1, -1)),
    ((1, 5, 3, 1), (2, 8, 3, -1)),
    ((6, 11, 2, 1), (8, 13, 2, -1)),
    ((11, 15, 1, 1), (14, 15, 1, -1)),
)


def parts_of(step, m):
    return (m,) if step == 3 else tuple(range(PARTS))


def dot(a, b, contract=(1, 0)):
    dims = (((contract[0],), (contract[1],)), ((), ()))
    return lax.dot_general(a, b, dims, preferred_element_type=F32)


def kernel(
    q_ref, p_ref, gt_ref, rows_ref, pos_ref,
    loss_ref, qg_ref, pg_ref,
    loss_v, qg_v, pg_v, pass_here, rows_here, topics, qall, posall, mat, mat_t, smat, smat_t, zbuf, ysend, picked,
    st, part, stats, row, wt,
    gsend, grecv, qpart, rssend, rsrecv, table, bsend, brecv, fin,
    local_sem, q_s, q_r, pos_s, pos_r, z_s, z_r, y_s, y_r,
    stat_s, stat_r, rs_s, rs_r, g_s, g_r, b_s, b_r, fin_s, fin_r,
):
    dp = lax.axis_index("dp")
    x = lax.axis_index("rep")
    z, e = dp // NE, dp % NE
    zs = {d: (lax.rem(z + d + NZ, NZ) * NE + e, x) for d in (-5, -1, 1, 5)}
    x_at = [lax.rem(x + o, NX) for o in range(NX)]
    e_at = [lax.rem(e + o, NE) for o in range(NE)]
    xs = [(dp, x_at[o]) for o in range(NX)]
    es = [(z * NE + e_at[o], x) for o in range(NE)]
    x_up, x_down = xs[1], xs[NX - 1]

    barrier = pltpu.get_barrier_semaphore()
    partners = list(zs.values()) + xs[1:] + es[1:]
    for partner in partners:
        pl.semaphore_signal(barrier, inc=1, device_id=partner, device_id_type=MESH)

    block = pl.ds(pl.multiple_of((dp // 16) * 128, 128), 128)
    loads = [
        pltpu.make_async_copy(src, dst, local_sem.at[n])
        for n, (src, dst) in enumerate(
            (
                (rows_ref.at[:, block], rows_here),
                (p_ref, pass_here),
                (gt_ref, topics),
                (q_ref, qall.at[x]),
                (pos_ref, posall.at[x]),
            )
        )
    ]
    for load in loads:
        load.start()

    started = []

    def send(src, dst, send_sem, recv_sem, to):
        copy = pltpu.make_async_remote_copy(
            src_ref=src, dst_ref=dst, send_sem=send_sem, recv_sem=recv_sem,
            device_id=to, device_id_type=MESH,
        )
        copy.start()
        started.append(copy)
        return copy

    def finish_sends():
        while started:
            started.pop(0).wait_send()

    lane = lax.broadcasted_iota(I32, (TOPICS, OWN), 1)
    first = (dp % 16) * 8
    loads[0].wait()
    here = rows_here[...] - dp * OWN

    def where_listed(i):
        col = jnp.sum(jnp.where(lane == first + i, here, 0).astype(F32), axis=1, keepdims=True)
        return jnp.where(lane.astype(F32) == col, 1.0, 0.0).astype(BF16)

    mine = jnp.concatenate([where_listed(x * SHARE + i) for i in range(SHARE)], axis=0)
    loads[1].wait()
    zbuf[0] = dot(mine, pass_here[...]).astype(BF16)
    for load in loads[2:]:
        load.wait()

    pl.semaphore_wait(barrier, len(partners))

    def sub(first, count, i):
        return pl.ds(first, count), pl.ds(i * 16, 16)

    zc = {}

    def spread(step, i):
        for m, (src, dst, count, far) in enumerate(STEPS[step]):
            if i in parts_of(step, m):
                zc[step, m, i] = send(
                    zbuf.at[sub(src, count, i)], zbuf.at[sub(dst, count, i)],
                    z_s.at[dst, i], z_r.at[dst, i], zs[far],
                )

    for i in range(PARTS):
        spread(0, i)

    qc, seen = {}, set()

    def got(copies, *keys):
        for key in keys:
            if (id(copies), key) not in seen:
                seen.add((id(copies), key))
                copies[key].wait_recv()

    def send_q(way, n):
        stage, i = divmod(n, PIECES)
        half = way if stage != 1 else 1 - way
        owner = x
        if stage == 2:
            owner = x_at[1] if way else x_at[3]
            got(qc, (way, i))
        rows = qall.at[owner, pl.ds(half * HALF + i * PIECE, PIECE)]
        qc[way, n] = send(rows, rows, q_s.at[way, n], q_r.at[way, n], x_down if way else x_up)

    def paced(send_piece, pace, h):
        for n in range(sum(pace[:h]), sum(pace[: h + 1])):
            send_piece(0, n)
            send_piece(1, n)

    paced(send_q, Q_PACE, 0)

    r16 = lax.broadcasted_iota(I32, (16, 256), 0)
    c256 = lax.broadcasted_iota(I32, (16, 256), 1)
    at = (r16 // 2) * BLOCK + (r16 % 2) * TOPICS
    for d in range(NE):
        chosen = at + topics[z * NE + d]
        smat[d * 16 : (d + 1) * 16, :] = jnp.where(c256 == chosen, 1.0, 0.0).astype(BF16)
    smat_t[...] = smat[...].T
    for i in range(8):
        mat[i * 16 : (i + 1) * 16, :] = where_listed(i)
    mat_t[...] = mat[...].T

    yc = {}

    def pick(ch):
        blocks = zbuf[ch * 8 : (ch + 1) * 8].reshape(256, D)
        ysend[ch] = dot(smat[...], blocks).astype(BF16).reshape(NE, 16, D)
        for o in FAR_FIRST:
            yc[ch, o] = send(
                ysend.at[ch, e_at[o]], picked.at[ch, e],
                y_s.at[ch, o - 1], y_r.at[ch, o - 1], es[o],
            )
        picked[ch, e] = ysend[ch, e]

    def receive(step):
        for i in range(PARTS):
            for m in range(len(STEPS[step])):
                if i in parts_of(step, m):
                    zc[step, m, i].wait_recv()
            if step < 3:
                spread(step + 1, i)

    receive(0)
    paced(send_q, Q_PACE, 1)
    pos_c = [
        send(posall.at[x], posall.at[x], pos_s.at[o - 1], pos_r.at[o - 1], xs[o])
        for o in range(1, NX)
    ]
    receive(1)
    paced(send_q, Q_PACE, 2)
    pick(0)
    receive(2)
    receive(3)
    pick(1)

    p = lax.broadcasted_iota(I32, (128, 1), 0)
    listed_at = []
    for ch in range(2):
        away = jnp.zeros((128, 1), I32)
        for n in range(8):
            away = jnp.where((p // 2) % 8 == n, ORDER[ch * 8 + n], away)
        z_of = (z + away + NZ) % NZ
        listed_at.append(z_of * 64 + (p // 16) * 8 + x * SHARE + p % 2)

    def columns(n):
        return pl.ds(pl.multiple_of(n * Q, Q), Q)

    def score(ch, n):
        cols = columns(n)
        s = dot(picked[ch].reshape(128, D), qall[n], (1, 1)) * (D ** -0.5)
        st[ch, :, cols] = s
        top = jnp.max(s, axis=0, keepdims=True)
        total = jnp.sum(jnp.exp(s - top), axis=0, keepdims=True)
        hot = listed_at[ch] == posall[n]
        hit = jnp.sum(jnp.where(hot, s, 0.0), axis=0, keepdims=True)
        for k, value in enumerate((top, total, hit)):
            for h in range(2):
                part[ch, k, pl.ds(n * 2 + h, 1), :] = value[:, h * 128 : (h + 1) * 128]

    for copy in pos_c:
        copy.wait_recv()
    for o in range(1, NE):
        yc[0, o].wait_recv()
    score(0, x_at[0])
    got(qc, *((0, n) for n in range(2 * PIECES)))
    score(0, x_at[3])
    got(qc, *((1, n) for n in range(2 * PIECES)))
    score(0, x_at[1])
    for o in range(1, NE):
        yc[1, o].wait_recv()
    for o in (0, 3, 1):
        score(1, x_at[o])
    got(qc, *((way, n) for way in range(2) for n in range(2 * PIECES, 3 * PIECES)))
    score(0, x_at[2])
    score(1, x_at[2])

    def merge(pieces):
        top = pieces[0][0]
        for piece in pieces[1:]:
            top = jnp.maximum(top, piece[0])
        total = sum(piece[1] * jnp.exp(piece[0] - top) for piece in pieces)
        return top, total, sum(piece[2] for piece in pieces)

    def pieces_of(ref, count):
        return [[ref[n, k] for k in range(3)] for n in range(count)]

    for k, value in enumerate(merge(pieces_of(part, 2))):
        stats[x, k] = value
    finish_fwd = list(started)
    started.clear()
    stat_c = [
        send(stats.at[x], stats.at[x], stat_s.at[o - 1], stat_r.at[o - 1], xs[o])
        for o in range(1, NX)
    ]
    for copy in finish_fwd:
        copy.wait_send()
    for copy in stat_c:
        copy.wait_recv()
    top, total, hit = merge(pieces_of(stats, NX))
    lse = top + jnp.log(total)
    row[0] = lse
    row[1] = lse - hit
    loss_v[...] = row[1, pl.ds(x * 2, 2), :]
    stores = [pltpu.make_async_copy(loss_v, loss_ref, local_sem.at[5])]
    stores[0].start()

    gc, rs = {}, {}

    def weigh(ch):
        for n in range(NX):
            cols = pl.ds(n * Q, Q)
            hot = jnp.where(listed_at[ch] == posall[n], 1.0, 0.0)
            lse = jnp.concatenate([row[0, 2 * n : 2 * n + 1, :], row[0, 2 * n + 1 : 2 * n + 2, :]], axis=1)
            wt[ch, :, cols] = (jnp.exp(st[ch, :, cols] - lse) - hot).astype(BF16)

    def term(ch):
        def tile(n, _):
            cols = pl.ds(pl.multiple_of(n * 256, 256), 256)
            g = dot(wt[ch], qall[:, :, cols].reshape(NX * Q, 256))
            gsend[ch, :, :, cols] = g.astype(BF16).reshape(NE, 16, 256)
            return 0

        lax.fori_loop(0, D // 256, tile, 0)
        for o in FAR_FIRST:
            gc[ch, o] = send(
                gsend.at[ch, e_at[o]], grecv.at[ch, e],
                g_s.at[ch, o - 1], g_r.at[ch, o - 1], es[o],
            )
        grecv[ch, e] = gsend[ch, e]

    def query_part(o):
        w = wt[:, :, columns(x_at[o])].reshape(256, Q).T

        def tile(n, _):
            out = pl.ds(pl.multiple_of(n * 256, 256), 256)
            qpart[o, :, out] = dot(w, picked[:, :, :, out].reshape(256, 256))
            return 0

        lax.fori_loop(0, D // 256, tile, 0)

    def send_rs(way, stage):
        for i in range(PIECES):
            half = way if stage == 1 else 1 - way
            rows = pl.ds(i * PIECE, PIECE)
            value = qpart[2 if stage == 0 else 3 if way else 1, pl.ds(half * HALF + i * PIECE, PIECE)]
            n = stage * PIECES + i
            if stage == 2:
                got(rs, (way, i))
                value = value + rsrecv[way, 0, rows].astype(F32)
            rssend[way, stage, rows] = value.astype(BF16)
            rs[way, n] = send(
                rssend.at[way, stage, rows], rsrecv.at[way, stage, rows],
                rs_s.at[way, n], rs_r.at[way, n], x_down if way else x_up,
            )

    weigh(1)
    term(1)
    weigh(0)
    query_part(2)
    send_rs(0, 0)
    send_rs(1, 0)
    query_part(1)
    send_rs(0, 1)
    query_part(3)
    send_rs(1, 1)
    term(0)

    def sum_by_topic(c):
        for o in range(1, NE):
            gc[c, o].wait_recv()
        sums = dot(smat_t[...], grecv[c].reshape(128, D))
        table[c * 8 : (c + 1) * 8] = sums.reshape(8, BLOCK, D)

    sum_by_topic(1)
    bc = {}

    def summed(first, count, i):
        values = [table[first + n, sub(0, 1, i)[1]] for n in range(count)]
        for step in range(1, 4):
            for m, (src, dst, width, _) in enumerate(STEPS[step]):
                held = [n for n in range(width) if first <= src + n < first + count]
                if held and i in parts_of(step, m):
                    if (step, m, i) not in seen:
                        seen.add((step, m, i))
                        bc[step, m, i].wait_recv()
                    for n in held:
                        more = brecv[dst + n, sub(0, 1, i)[1]].astype(F32)
                        values[src + n - first] = values[src + n - first] + more
        return values

    def send_back(step):
        for i in range(PARTS):
            for m, (_, dst, count, far) in enumerate(STEPS[step]):
                if i in parts_of(step, m):
                    for n, value in enumerate(summed(dst, count, i)):
                        bsend[dst + n, sub(0, 1, i)[1]] = value.astype(BF16)
                    bc[step, m, i] = send(
                        bsend.at[sub(dst, count, i)], brecv.at[sub(dst, count, i)],
                        b_s.at[dst, i], b_r.at[dst, i], zs[-far],
                    )

    send_back(3)
    send_back(2)
    sum_by_topic(0)
    send_rs(0, 2)
    send_rs(1, 2)
    send_back(1)
    send_back(0)
    fin_c = []
    for i in range(PARTS):
        rows = sub(0, 1, i)[1]
        value = table[0, rows]
        for m, (_, dst, _, _) in enumerate(STEPS[0]):
            bc[0, m, i].wait_recv()
            value = value + brecv[dst, rows].astype(F32)
        fin[x, rows] = value.astype(BF16)
        for o in range(1, NX):
            here = fin.at[x, rows]
            fin_c.append(send(here, here, fin_s.at[o - 1, i], fin_r.at[o - 1, i], xs[o]))
    query_part(0)
    got(rs, *((way, n) for n in range(PIECES, 3 * PIECES) for way in range(2)))
    for half in range(2):
        rows = pl.ds(half * HALF, HALF)
        value = qpart[0, rows] + rsrecv[half, 1].astype(F32) + rsrecv[1 - half, 2].astype(F32)
        qg_v[rows] = value.astype(BF16)
    stores.append(pltpu.make_async_copy(qg_v, qg_ref, local_sem.at[6]))
    stores[1].start()
    for copy in fin_c:
        copy.wait_recv()
    pg_v[...] = dot(mat_t[...], fin[...].reshape(OWN, D)).astype(BF16)
    stores.append(pltpu.make_async_copy(pg_v, pg_ref, local_sem.at[7]))
    stores[2].start()
    finish_sends()
    for store in stores:
        store.wait()


def shards(queries, passages, group_topic, topic_rows, positive):
    hbm = pl.BlockSpec(memory_space=pltpu.HBM)
    dma = pltpu.SemaphoreType.DMA
    loss, query_grad, passage_grad = pl.pallas_call(
        kernel,
        out_shape=(
            jax.ShapeDtypeStruct((2, 128), F32),
            jax.ShapeDtypeStruct((Q, D), BF16),
            jax.ShapeDtypeStruct((OWN, D), BF16),
        ),
        in_specs=[hbm] * 5,
        out_specs=(hbm, hbm, hbm),
        scratch_shapes=[
            pltpu.VMEM((2, 128), F32),
            pltpu.VMEM((Q, D), BF16),
            pltpu.VMEM((OWN, D), BF16),
            pltpu.VMEM((OWN, D), BF16),
            pltpu.VMEM((TOPICS, 128), I32),
            pltpu.SMEM((128,), I32),
            pltpu.VMEM((NX, Q, D), BF16),
            pltpu.VMEM((NX, 1, Q), I32),
            pltpu.VMEM((OWN, OWN), BF16),
            pltpu.VMEM((OWN, OWN), BF16),
            pltpu.VMEM((128, 256), BF16),
            pltpu.VMEM((256, 128), BF16),
            pltpu.VMEM((NZ, BLOCK, D), BF16),
            pltpu.VMEM((2, NE, 16, D), BF16),
            pltpu.VMEM((2, NE, 16, D), BF16),
            pltpu.VMEM((2, 128, NX * Q), F32),
            pltpu.VMEM((2, 3, 8, 128), F32),
            pltpu.VMEM((NX, 3, 8, 128), F32),
            pltpu.VMEM((2, 8, 128), F32),
            pltpu.VMEM((2, 128, NX * Q), BF16),
            pltpu.VMEM((2, NE, 16, D), BF16),
            pltpu.VMEM((2, NE, 16, D), BF16),
            pltpu.VMEM((NX, Q, D), F32),
            pltpu.VMEM((2, 3, HALF, D), BF16),
            pltpu.VMEM((2, 3, HALF, D), BF16),
            pltpu.VMEM((NZ, BLOCK, D), F32),
            pltpu.VMEM((NZ, BLOCK, D), BF16),
            pltpu.VMEM((NZ, BLOCK, D), BF16),
            pltpu.VMEM((NX, BLOCK, D), BF16),
            dma((8,)),
            dma((2, 3 * PIECES)), dma((2, 3 * PIECES)), dma((3,)), dma((3,)),
            dma((NZ, PARTS)), dma((NZ, PARTS)),
            dma((2, NE - 1)), dma((2, NE - 1)),
            dma((3,)), dma((3,)), dma((2, 3 * PIECES)), dma((2, 3 * PIECES)),
            dma((2, NE - 1)), dma((2, NE - 1)),
            dma((NZ, PARTS)), dma((NZ, PARTS)),
            dma((3, PARTS)), dma((3, PARTS)),
        ],
        compiler_params=pltpu.CompilerParams(
            collective_id=0, has_side_effects=True, vmem_limit_bytes=60 * 1024 * 1024
        ),
        cost_estimate=pl.CostEstimate(
            flops=3 * 2 * 256 * 1024 * 1024, bytes_accessed=2 * 1024 * 1024, transcendentals=2 * 256 * 1024
        ),
    )(queries, passages, group_topic, topic_rows, positive.reshape(1, Q))
    return loss.reshape(Q), query_grad, passage_grad


def solution(mesh):
    return jax.shard_map(
        shards,
        mesh=mesh,
        in_specs=(P(("dp", "rep"), None), P("dp", None), P(), P(), P(("dp", "rep"))),
        out_specs=(P(("dp", "rep")), P(("dp", "rep"), None), P("dp", None)),
        check_vma=False,
    )
```

```python
import jax
import jax.numpy as jnp
from jax import lax
from jax.experimental import pallas as pl
from jax.experimental.pallas import tpu as pltpu
from jax.sharding import PartitionSpec as P

F32, BF16, I32 = jnp.float32, jnp.bfloat16, jnp.int32
MESH = pl.DeviceIdType.MESH
D = 1024
Q = 256
OWN = 128
TOPICS = 16
NZ, NE, NX = 16, 8, 4
SHARE = 2
BLOCK = SHARE * TOPICS
HALF = 128
PARTS = 2
Q_PACE = (1, 1, 1)
PIECES, PIECE = 1, 128

ORDER = (0, -1, -5, 5, 1, -2, -6, 4, -4, 6, 2, -7, 3, -3, 7, 8)
STEPS = (
    ((0, 2, 1, 5), (0, 3, 1, -5), (0, 1, 1, 1), (0, 4, 1, -1)),
    ((1, 5, 3, 1), (2, 8, 3, -1)),
    ((6, 11, 2, 1), (8, 13, 2, -1)),
    ((11, 15, 1, 1), (14, 15, 1, -1)),
)


def parts_of(step, m):
    return (m,) if step == 3 else tuple(range(PARTS))


def dot(a, b, contract=(1, 0)):
    dims = (((contract[0],), (contract[1],)), ((), ()))
    return lax.dot_general(a, b, dims, preferred_element_type=F32)


def kernel(
    q_ref, p_ref, gt_ref, rows_ref, pos_ref,
    loss_ref, qg_ref, pg_ref,
    loss_v, qg_v, pg_v, pass_here, rows_here, topics, qall, posall, mat, mat_t, smat, smat_t, zbuf, ysend, picked,
    st, part, stats, row, wt,
    gsend, grecv, qpart, rssend, rsrecv, table, bsend, brecv, fin,
    local_sem, q_s, q_r, pos_s, pos_r, z_s, z_r, y_s, y_r,
    stat_s, stat_r, rs_s, rs_r, g_s, g_r, b_s, b_r, fin_s, fin_r,
):
    dp = lax.axis_index("dp")
    x = lax.axis_index("rep")
    z, e = dp // NE, dp % NE
    zs = {d: (lax.rem(z + d + NZ, NZ) * NE + e, x) for d in (-5, -1, 1, 5)}
    x_at = [lax.rem(x + o, NX) for o in range(NX)]
    e_at = [lax.rem(e + o, NE) for o in range(NE)]
    xs = [(dp, x_at[o]) for o in range(NX)]
    es = [(z * NE + e_at[o], x) for o in range(NE)]
    x_up, x_down = xs[1], xs[NX - 1]

    barrier = pltpu.get_barrier_semaphore()
    partners = list(zs.values()) + xs[1:] + es[1:]
    for partner in partners:
        pl.semaphore_signal(barrier, inc=1, device_id=partner, device_id_type=MESH)

    block = pl.ds(pl.multiple_of((dp // 16) * 128, 128), 128)
    loads = [
        pltpu.make_async_copy(src, dst, local_sem.at[n])
        for n, (src, dst) in enumerate(
            (
                (rows_ref.at[:, block], rows_here),
                (p_ref, pass_here),
                (gt_ref, topics),
                (q_ref, qall.at[x]),
                (pos_ref, posall.at[x]),
            )
        )
    ]
    for load in loads:
        load.start()

    started = []

    def send(src, dst, send_sem, recv_sem, to):
        copy = pltpu.make_async_remote_copy(
            src_ref=src, dst_ref=dst, send_sem=send_sem, recv_sem=recv_sem,
            device_id=to, device_id_type=MESH,
        )
        copy.start()
        started.append(copy)
        return copy

    def finish_sends():
        while started:
            started.pop(0).wait_send()

    lane = lax.broadcasted_iota(I32, (TOPICS, OWN), 1)
    first = (dp % 16) * 8
    loads[0].wait()
    here = rows_here[...] - dp * OWN
    for i in range(8):
        col = jnp.sum(jnp.where(lane == first + i, here, 0).astype(F32), axis=1, keepdims=True)
        mat[i * 16 : (i + 1) * 16, :] = jnp.where(lane.astype(F32) == col, 1.0, 0.0).astype(BF16)
    mine = mat[pl.ds(pl.multiple_of(x * BLOCK, BLOCK), BLOCK), :]
    loads[1].wait()
    zbuf[0] = dot(mine, pass_here[...]).astype(BF16)
    for load in loads[2:]:
        load.wait()

    pl.semaphore_wait(barrier, len(partners))

    def sub(first, count, i):
        return pl.ds(first, count), pl.ds(i * 16, 16)

    zc = {}

    def spread(step, i):
        for m, (src, dst, count, far) in enumerate(STEPS[step]):
            if i in parts_of(step, m):
                zc[step, m, i] = send(
                    zbuf.at[sub(src, count, i)], zbuf.at[sub(dst, count, i)],
                    z_s.at[dst, i], z_r.at[dst, i], zs[far],
                )

    for i in range(PARTS):
        spread(0, i)

    qc, seen = {}, set()

    def got(copies, *keys):
        for key in keys:
            if (id(copies), key) not in seen:
                seen.add((id(copies), key))
                copies[key].wait_recv()

    def send_q(way, n):
        stage, i = divmod(n, PIECES)
        half = way if stage != 1 else 1 - way
        owner = x
        if stage == 2:
            owner = x_at[1] if way else x_at[3]
            got(qc, (way, i))
        rows = qall.at[owner, pl.ds(half * HALF + i * PIECE, PIECE)]
        qc[way, n] = send(rows, rows, q_s.at[way, n], q_r.at[way, n], x_down if way else x_up)

    def paced(send_piece, pace, h):
        for n in range(sum(pace[:h]), sum(pace[: h + 1])):
            send_piece(0, n)
            send_piece(1, n)

    paced(send_q, Q_PACE, 0)

    r16 = lax.broadcasted_iota(I32, (16, 256), 0)
    c256 = lax.broadcasted_iota(I32, (16, 256), 1)
    at = (r16 // 2) * BLOCK + (r16 % 2) * TOPICS
    for d in range(NE):
        chosen = at + topics[z * NE + d]
        smat[d * 16 : (d + 1) * 16, :] = jnp.where(c256 == chosen, 1.0, 0.0).astype(BF16)
    smat_t[...] = smat[...].T
    mat_t[...] = mat[...].T

    yc = {}

    def pick(ch):
        blocks = zbuf[ch * 8 : (ch + 1) * 8].reshape(256, D)
        ysend[ch] = dot(smat[...], blocks).astype(BF16).reshape(NE, 16, D)
        for o in range(1, NE):
            yc[ch, o] = send(
                ysend.at[ch, e_at[o]], picked.at[ch, e],
                y_s.at[ch, o - 1], y_r.at[ch, o - 1], es[o],
            )
        picked[ch, e] = ysend[ch, e]

    def receive(step):
        for i in range(PARTS):
            for m in range(len(STEPS[step])):
                if i in parts_of(step, m):
                    zc[step, m, i].wait_recv()
            if step < 3:
                spread(step + 1, i)

    receive(0)
    paced(send_q, Q_PACE, 1)
    pos_c = [
        send(posall.at[x], posall.at[x], pos_s.at[o - 1], pos_r.at[o - 1], xs[o])
        for o in range(1, NX)
    ]
    receive(1)
    paced(send_q, Q_PACE, 2)
    pick(0)
    receive(2)
    receive(3)
    pick(1)

    p = lax.broadcasted_iota(I32, (128, 1), 0)
    listed_at = []
    for ch in range(2):
        away = jnp.zeros((128, 1), I32)
        for n in range(8):
            away = jnp.where((p // 2) % 8 == n, ORDER[ch * 8 + n], away)
        z_of = (z + away + NZ) % NZ
        listed_at.append(z_of * 64 + (p // 16) * 8 + x * SHARE + p % 2)

    def columns(n):
        return pl.ds(pl.multiple_of(n * Q, Q), Q)

    def score(ch, n):
        cols = columns(n)
        s = dot(picked[ch].reshape(128, D), qall[n], (1, 1)) * (D ** -0.5)
        st[ch, :, cols] = s
        top = jnp.max(s, axis=0, keepdims=True)
        total = jnp.sum(jnp.exp(s - top), axis=0, keepdims=True)
        hot = listed_at[ch] == posall[n]
        hit = jnp.sum(jnp.where(hot, s, 0.0), axis=0, keepdims=True)
        for k, value in enumerate((top, total, hit)):
            for h in range(2):
                part[ch, k, pl.ds(n * 2 + h, 1), :] = value[:, h * 128 : (h + 1) * 128]

    for copy in pos_c:
        copy.wait_recv()
    for o in range(1, NE):
        yc[0, o].wait_recv()
    score(0, x_at[0])
    got(qc, *((0, n) for n in range(2 * PIECES)))
    score(0, x_at[3])
    got(qc, *((1, n) for n in range(2 * PIECES)))
    score(0, x_at[1])
    for o in range(1, NE):
        yc[1, o].wait_recv()
    for o in (0, 3, 1):
        score(1, x_at[o])
    got(qc, *((way, n) for way in range(2) for n in range(2 * PIECES, 3 * PIECES)))
    score(0, x_at[2])
    score(1, x_at[2])

    def merge(pieces):
        top = pieces[0][0]
        for piece in pieces[1:]:
            top = jnp.maximum(top, piece[0])
        total = sum(piece[1] * jnp.exp(piece[0] - top) for piece in pieces)
        return top, total, sum(piece[2] for piece in pieces)

    def pieces_of(ref, count):
        return [[ref[n, k] for k in range(3)] for n in range(count)]

    for k, value in enumerate(merge(pieces_of(part, 2))):
        stats[x, k] = value
    finish_fwd = list(started)
    started.clear()
    stat_c = [
        send(stats.at[x], stats.at[x], stat_s.at[o - 1], stat_r.at[o - 1], xs[o])
        for o in range(1, NX)
    ]
    for copy in finish_fwd:
        copy.wait_send()
    for copy in stat_c:
        copy.wait_recv()
    top, total, hit = merge(pieces_of(stats, NX))
    lse = top + jnp.log(total)
    row[0] = lse
    row[1] = lse - hit
    loss_v[...] = row[1, pl.ds(x * 2, 2), :]
    stores = [pltpu.make_async_copy(loss_v, loss_ref, local_sem.at[5])]
    stores[0].start()

    gc, rs = {}, {}

    def weigh(ch):
        for n in range(NX):
            cols = pl.ds(n * Q, Q)
            hot = jnp.where(listed_at[ch] == posall[n], 1.0, 0.0)
            lse = jnp.concatenate([row[0, 2 * n : 2 * n + 1, :], row[0, 2 * n + 1 : 2 * n + 2, :]], axis=1)
            wt[ch, :, cols] = (jnp.exp(st[ch, :, cols] - lse) - hot).astype(BF16)

    def term(ch):
        def tile(n, _):
            cols = pl.ds(pl.multiple_of(n * 256, 256), 256)
            g = dot(wt[ch], qall[:, :, cols].reshape(NX * Q, 256))
            gsend[ch, :, :, cols] = g.astype(BF16).reshape(NE, 16, 256)
            return 0

        lax.fori_loop(0, D // 256, tile, 0)
        for o in range(1, NE):
            gc[ch, o] = send(
                gsend.at[ch, e_at[o]], grecv.at[ch, e],
                g_s.at[ch, o - 1], g_r.at[ch, o - 1], es[o],
            )
        grecv[ch, e] = gsend[ch, e]

    def query_part(o):
        w = wt[:, :, columns(x_at[o])].reshape(256, Q).T

        def tile(n, _):
            out = pl.ds(pl.multiple_of(n * 256, 256), 256)
            qpart[o, :, out] = dot(w, picked[:, :, :, out].reshape(256, 256))
            return 0

        lax.fori_loop(0, D // 256, tile, 0)

    def send_rs(way, stage):
        for i in range(PIECES):
            half = way if stage == 1 else 1 - way
            rows = pl.ds(i * PIECE, PIECE)
            value = qpart[2 if stage == 0 else 3 if way else 1, pl.ds(half * HALF + i * PIECE, PIECE)]
            n = stage * PIECES + i
            if stage == 2:
                got(rs, (way, i))
                value = value + rsrecv[way, 0, rows].astype(F32)
            rssend[way, stage, rows] = value.astype(BF16)
            rs[way, n] = send(
                rssend.at[way, stage, rows], rsrecv.at[way, stage, rows],
                rs_s.at[way, n], rs_r.at[way, n], x_down if way else x_up,
            )

    weigh(1)
    term(1)
    weigh(0)
    query_part(2)
    send_rs(0, 0)
    send_rs(1, 0)
    query_part(1)
    send_rs(0, 1)
    query_part(3)
    send_rs(1, 1)
    term(0)

    def sum_by_topic(c):
        for o in range(1, NE):
            gc[c, o].wait_recv()
        sums = dot(smat_t[...], grecv[c].reshape(128, D))
        table[c * 8 : (c + 1) * 8] = sums.reshape(8, BLOCK, D)

    sum_by_topic(1)
    bc = {}

    def summed(first, count, i):
        values = [table[first + n, sub(0, 1, i)[1]] for n in range(count)]
        for step in range(1, 4):
            for m, (src, dst, width, _) in enumerate(STEPS[step]):
                held = [n for n in range(width) if first <= src + n < first + count]
                if held and i in parts_of(step, m):
                    if (step, m, i) not in seen:
                        seen.add((step, m, i))
                        bc[step, m, i].wait_recv()
                    for n in held:
                        more = brecv[dst + n, sub(0, 1, i)[1]].astype(F32)
                        values[src + n - first] = values[src + n - first] + more
        return values

    def send_back(step):
        for i in range(PARTS):
            for m, (_, dst, count, far) in enumerate(STEPS[step]):
                if i in parts_of(step, m):
                    for n, value in enumerate(summed(dst, count, i)):
                        bsend[dst + n, sub(0, 1, i)[1]] = value.astype(BF16)
                    bc[step, m, i] = send(
                        bsend.at[sub(dst, count, i)], brecv.at[sub(dst, count, i)],
                        b_s.at[dst, i], b_r.at[dst, i], zs[-far],
                    )

    send_back(3)
    send_back(2)
    sum_by_topic(0)
    send_back(1)
    send_rs(0, 2)
    send_rs(1, 2)
    send_back(0)
    fin_c = []
    for i in range(PARTS):
        rows = sub(0, 1, i)[1]
        value = table[0, rows]
        for m, (_, dst, _, _) in enumerate(STEPS[0]):
            bc[0, m, i].wait_recv()
            value = value + brecv[dst, rows].astype(F32)
        fin[x, rows] = value.astype(BF16)
        for o in range(1, NX):
            here = fin.at[x, rows]
            fin_c.append(send(here, here, fin_s.at[o - 1, i], fin_r.at[o - 1, i], xs[o]))
    query_part(0)
    got(rs, *((way, n) for n in range(PIECES, 3 * PIECES) for way in range(2)))
    for half in range(2):
        rows = pl.ds(half * HALF, HALF)
        value = qpart[0, rows] + rsrecv[half, 1].astype(F32) + rsrecv[1 - half, 2].astype(F32)
        qg_v[rows] = value.astype(BF16)
    stores.append(pltpu.make_async_copy(qg_v, qg_ref, local_sem.at[6]))
    stores[1].start()
    for copy in fin_c:
        copy.wait_recv()
    pg_v[...] = dot(mat_t[...], fin[...].reshape(OWN, D)).astype(BF16)
    stores.append(pltpu.make_async_copy(pg_v, pg_ref, local_sem.at[7]))
    stores[2].start()
    finish_sends()
    for store in stores:
        store.wait()


def shards(queries, passages, group_topic, topic_rows, positive):
    hbm = pl.BlockSpec(memory_space=pltpu.HBM)
    dma = pltpu.SemaphoreType.DMA
    loss, query_grad, passage_grad = pl.pallas_call(
        kernel,
        out_shape=(
            jax.ShapeDtypeStruct((2, 128), F32),
            jax.ShapeDtypeStruct((Q, D), BF16),
            jax.ShapeDtypeStruct((OWN, D), BF16),
        ),
        in_specs=[hbm] * 5,
        out_specs=(hbm, hbm, hbm),
        scratch_shapes=[
            pltpu.VMEM((2, 128), F32),
            pltpu.VMEM((Q, D), BF16),
            pltpu.VMEM((OWN, D), BF16),
            pltpu.VMEM((OWN, D), BF16),
            pltpu.VMEM((TOPICS, 128), I32),
            pltpu.SMEM((128,), I32),
            pltpu.VMEM((NX, Q, D), BF16),
            pltpu.VMEM((NX, 1, Q), I32),
            pltpu.VMEM((OWN, OWN), BF16),
            pltpu.VMEM((OWN, OWN), BF16),
            pltpu.VMEM((128, 256), BF16),
            pltpu.VMEM((256, 128), BF16),
            pltpu.VMEM((NZ, BLOCK, D), BF16),
            pltpu.VMEM((2, NE, 16, D), BF16),
            pltpu.VMEM((2, NE, 16, D), BF16),
            pltpu.VMEM((2, 128, NX * Q), F32),
            pltpu.VMEM((2, 3, 8, 128), F32),
            pltpu.VMEM((NX, 3, 8, 128), F32),
            pltpu.VMEM((2, 8, 128), F32),
            pltpu.VMEM((2, 128, NX * Q), BF16),
            pltpu.VMEM((2, NE, 16, D), BF16),
            pltpu.VMEM((2, NE, 16, D), BF16),
            pltpu.VMEM((NX, Q, D), F32),
            pltpu.VMEM((2, 3, HALF, D), BF16),
            pltpu.VMEM((2, 3, HALF, D), BF16),
            pltpu.VMEM((NZ, BLOCK, D), F32),
            pltpu.VMEM((NZ, BLOCK, D), BF16),
            pltpu.VMEM((NZ, BLOCK, D), BF16),
            pltpu.VMEM((NX, BLOCK, D), BF16),
            dma((8,)),
            dma((2, 3 * PIECES)), dma((2, 3 * PIECES)), dma((3,)), dma((3,)),
            dma((NZ, PARTS)), dma((NZ, PARTS)),
            dma((2, NE - 1)), dma((2, NE - 1)),
            dma((3,)), dma((3,)), dma((2, 3 * PIECES)), dma((2, 3 * PIECES)),
            dma((2, NE - 1)), dma((2, NE - 1)),
            dma((NZ, PARTS)), dma((NZ, PARTS)),
            dma((3, PARTS)), dma((3, PARTS)),
        ],
        compiler_params=pltpu.CompilerParams(
            collective_id=0, has_side_effects=True, vmem_limit_bytes=60 * 1024 * 1024
        ),
        cost_estimate=pl.CostEstimate(
            flops=3 * 2 * 256 * 1024 * 1024, bytes_accessed=2 * 1024 * 1024, transcendentals=2 * 256 * 1024
        ),
    )(queries, passages, group_topic, topic_rows, positive.reshape(1, Q))
    return loss.reshape(Q), query_grad, passage_grad


def solution(mesh):
    return jax.shard_map(
        shards,
        mesh=mesh,
        in_specs=(P(("dp", "rep"), None), P("dp", None), P(), P(), P(("dp", "rep"))),
        out_specs=(P(("dp", "rep")), P(("dp", "rep"), None), P("dp", None)),
        check_vma=False,
    )
```
